32 devices in a mesh: groups: 2 (over x), tensor: 8 (over z, y), request: 2 (over core).
Axes of the slice: x: 2, y: 2, z: 4, core: 2. Of those that a mesh axis runs over, the one named last changes fastest.
Arguments:
- queries: bfloat16 [256, 1024], P(('groups', 'request'), 'tensor'), parts along dimension 0, may hold values from -120 to 120
- fresh_kv: bfloat16 [2, 256, 1024], P(None, ('groups', 'request'), 'tensor'), parts along dimension 1, may hold values from -5 to 5
- kv_cache: bfloat16 [2, 256, 128, 1024], P(None, ('groups', 'request'), None, 'tensor'), parts along dimension 1, may hold values from -5 to 5
- lengths: int32 [256], P(('groups', 'request')), parts along dimension 0, may hold values from 16 to 128, as said below
- stream: bfloat16 [256, 6144], P(('groups', 'request'), 'tensor'), parts along dimension 0, may hold values from -6 to 6
- out_weight: bfloat16 [1024, 6144], P('tensor'), may hold values from -0.25 to 0.25
- block_ids: int32 [256, 3], P('groups'), parts along dimension 0, may hold values from 0 to 31, all different within a row; in each aligned block of 128 rows (0 to 127, 128 to 255, ...) at most 48 rows name the same one
- up_weight: bfloat16 [6144, 4096], P(None, ('tensor', 'request')), may hold values from -0.078125 to 0.078125
- down_weight: bfloat16 [4096, 6144], P(('tensor', 'request')), may hold values from -0.3125 to 0.3125
Outputs:
- layer_out: bfloat16 [256, 6144], P(('groups', 'request'), 'tensor'), parts along dimension 0
The draws below stay inside these ranges and needn't reach their ends.
There are 2 independent parts, one for each index of `groups`. The reference program is written for one: setup_inputs(seed, part) draws one part's arguments, and reference() takes and returns one part's arrays. A program takes and returns all parts, laid end to end along the dimension named above; an argument that names none is the same for every part. Nothing has to cross between parts.
Inputs may be any that keep to these rules, and one draw needn't show every extreme that they name: `block_ids`: each row names 3 different blocks; every block is named by some row; no block is named by more than 48 rows of the batch, and some block by exactly 48. `lengths`: some row of the batch uses all 128 positions.
All inputs are finite; a program needn't handle non-finite values.
Results may differ from the reference program's by a relative error of at most 0.0055.
Values may be sent and summed in bfloat16 or wider, within the bound.
No kernel may reach another device: no remote copies, remote signals or barrier semaphores. Data moves between devices by JAX's collectives and lax.ppermute only.
A program may use at most 64 MiB of HBM per device.

```python
import math
import jax
import jax.numpy as jnp
import numpy as np
from jax import lax

D = 6144
HS = 128
HEADS = 8
BLOCK = 128
NBLK = 32
FF = 4096
ACT = 3
ROWS = 128
CAP = 48
CACHE = 128


def shared_parts(key):
    first_keys = jnp.clip(jax.random.normal(jax.random.fold_in(key, 103), (ROWS, HEADS * HS)), -4.0, 4.0)
    return first_keys


def draw_queries(key, part):
    key = jax.random.fold_in(key, 1)
    values = jnp.clip(jax.random.normal(key, (ROWS, HEADS * HS)), -5.0, 5.0)
    return values.astype(jnp.bfloat16)


def draw_kv_cache(key, part):
    first_keys = shared_parts(key)
    key = jax.random.fold_in(key, 2)
    values = jnp.clip(jax.random.normal(key, (2, ROWS, CACHE, HEADS * HS)), -5.0, 5.0)
    values = values.at[0, :, 0, :].set(first_keys)
    return values.astype(jnp.bfloat16)


def draw_lengths(key, part):
    key = jax.random.fold_in(key, 3)
    counts = jax.random.randint(key, (ROWS,), CACHE // 8, CACHE + 1)
    picked = jax.random.randint(jax.random.fold_in(key, 4), (), 0, ROWS)
    return counts.at[picked].set(CACHE).astype(jnp.int32)


def steps_of(key, dims, cuts, low, top_value):
    def one(dim, shards_of):
        draws = jax.random.uniform(jax.random.fold_in(jax.random.fold_in(key, 6), dim), (shards_of,), jnp.float32, low / len(cuts), top_value / len(cuts))
        return jnp.repeat(jnp.exp(draws), dims[dim] // shards_of).reshape((-1,) + (1,) * (len(dims) - dim - 1))

    loudness = one(*cuts[0])
    for cut in cuts[1:]:
        loudness = loudness * one(*cut)
    return loudness


def shared_out(key, own, number, rows, amount, top, reach, lean):
    sequence = jax.random.permutation(key, amount)
    heavy_load, ordinary = load_shares(amount, rows * top, reach, lean, True), load_shares(amount, rows * top, reach, lean, False)
    places = jnp.arange(amount)

    def named(sizes, offset_by):
        used = int((sizes > 0).sum())
        fixed = max(1, used // 4)
        passed = fixed + (places - fixed + offset_by * (used - fixed)) % max(1, amount - fixed)
        return jnp.zeros((amount,), jnp.int32).at[sequence[jnp.where(places < fixed, places, passed)]].set(jnp.asarray(sizes, jnp.int32))

    sizes = jnp.where(number % 4 == 0, named(heavy_load, number // 4), named(ordinary, number - number // 4 - 1))
    mixed = jax.random.permutation(jax.random.fold_in(own, 3), amount)
    giver, receiver = mixed[0:amount // 2 * 2:2], mixed[1:amount // 2 * 2:2]
    room = jnp.minimum(sizes[giver] - 1, reach - sizes[receiver]) // 2
    room = jnp.where((giver == sequence[0]) | (receiver == sequence[0]) | (sizes[receiver] == 0), 0, jnp.maximum(room, 0))
    passed = jax.random.randint(jax.random.fold_in(own, 4), (amount // 2,), 0, 1 << 20) % (room + 1)
    sizes = sizes.at[giver].add(-passed).at[receiver].add(passed)
    items = jnp.searchsorted(jnp.cumsum(sizes), jnp.arange(rows * top), side="right").astype(jnp.int32)
    listing = items.reshape(top, rows).T
    listing = listing[jax.random.permutation(jax.random.fold_in(own, 1), rows)]
    offset_by = jax.random.randint(jax.random.fold_in(own, 2), (rows, 1), 0, top)
    return jnp.take_along_axis(listing, (jnp.arange(top)[None, :] + offset_by) % top, axis=1)


def load_shares(number_of, total, reach, skew, full):
    portions = [(1 << 20) // math.isqrt(rank ** skew) + 1 for rank in range(1, number_of + 1)]
    largest = reach if full else min(reach, max(-(-total // number_of), total * portions[0] // sum(portions)))
    least = 1 if total - largest >= number_of - 1 else 0
    holding, spare = [largest] + [least] * (number_of - 1), total - largest - least * (number_of - 1)
    while spare > 0:
        candidates = [i for i in range(1, number_of) if holding[i] < largest] or [i for i in range(1, number_of) if holding[i] < reach]
        pool, left = sum([portions[i] for i in candidates]), spare
        for i in candidates:
            extra = min(reach - holding[i], max(1, left * portions[i] // pool), spare)
            holding[i] = holding[i] + extra
            spare = spare - extra
    return np.array(holding)


def gaussian(key, dims, width, most, cuts=(), kind=jnp.bfloat16):
    values = jax.random.normal(key, dims, jnp.float32) * width
    if len(cuts) > 0:
        values = steps_of(key, dims, cuts, -0.22, 0.18) * values
    return jnp.clip(values, min=-most, max=most).astype(kind)


def setup_inputs(seed: int = 0, part: int = 0) -> dict:
    key_list = jax.random.split(jax.random.key(seed), 10)
    part_splits = jax.random.split(jax.random.fold_in(key_list[9], part), 10)
    queries = draw_queries(jax.random.fold_in(jax.random.fold_in(key_list[9], part), 71), part)
    fresh_kv = gaussian(part_splits[1], (2, ROWS, HEADS * HS), 1.0, 5.0, ((1, 2), (2, 8)))
    kv_cache = draw_kv_cache(jax.random.fold_in(jax.random.fold_in(key_list[9], part), 71), part)
    lengths = draw_lengths(jax.random.fold_in(jax.random.fold_in(key_list[9], part), 71), part)
    stream = gaussian(part_splits[4], (ROWS, D), 1.0, 6.0, ((0, 2), (1, 8)))
    out_weight = gaussian(key_list[5], (HEADS * HS, D), (HS * 4) ** -0.5, 0.25, ((0, 8),))
    block_ids_keys = jax.random.split(jax.random.fold_in(part_splits[6], 1), ROWS // ROWS)
    block_ids_turns = jax.random.permutation(jax.random.fold_in(part_splits[6], 3), ROWS // ROWS)
    block_ids = jax.vmap(lambda own, number: shared_out(jax.random.fold_in(part_splits[6], 2), own, number, ROWS, NBLK, ACT, CAP, 2))(block_ids_keys, block_ids_turns).reshape((ROWS, ACT))
    up_weight = gaussian(key_list[7], (D, FF), D ** -0.5, 0.078125, ((1, 16),))
    down_weight = gaussian(key_list[8], (FF, D), (ACT * BLOCK) ** -0.5, 0.3125, ((0, 16),))
    return dict(queries=queries, fresh_kv=fresh_kv, kv_cache=kv_cache, lengths=lengths, stream=stream, out_weight=out_weight, block_ids=block_ids, up_weight=up_weight, down_weight=down_weight)


def attend_single(items):
    query_row, key_new, value_new, cache_keys, cache_values, length = items
    shaped_q = query_row.astype(jnp.float32).reshape(HEADS, HS)
    keys_f = cache_keys.astype(jnp.float32).reshape(CACHE, HEADS, HS)
    values_f = cache_values.astype(jnp.float32).reshape(CACHE, HEADS, HS)
    scale = 1.0 / math.sqrt(HS)
    scores = jnp.einsum('hd,phd->hp', shaped_q, keys_f) * scale
    positions = jnp.arange(CACHE)
    scores = jnp.where(positions[None, :] < length, scores, -jnp.inf)
    own_score = lax.optimization_barrier(jnp.sum(shaped_q * key_new.astype(jnp.float32).reshape(HEADS, HS), axis=1)) * scale
    top = jnp.maximum(lax.optimization_barrier(jnp.max(scores, axis=1)), own_score)
    weights = jnp.exp(scores - top[:, None])
    own_weight = jnp.exp(own_score - top)
    total = lax.optimization_barrier(jnp.sum(weights, axis=1)) + own_weight
    probs = (weights / total[:, None]).astype(jnp.bfloat16)
    own_prob = (own_weight / total).astype(jnp.bfloat16)
    result = jnp.einsum('hp,phd->hd', probs.astype(jnp.float32), values_f)
    result = result + own_prob.astype(jnp.float32)[:, None] * value_new.astype(jnp.float32).reshape(HEADS, HS)
    return result.astype(jnp.bfloat16).reshape(HEADS * HS)

def reference(queries, fresh_kv, kv_cache, lengths, stream, out_weight, block_ids, up_weight, down_weight):
    attended = lax.map(attend_single, (queries, fresh_kv[0], fresh_kv[1], kv_cache[0], kv_cache[1], lengths))
    mixed = stream.astype(jnp.float32) + jnp.dot(attended, out_weight, preferred_element_type=jnp.float32)
    center = lax.optimization_barrier(jnp.mean(mixed, axis=1, keepdims=True))
    spread = lax.optimization_barrier(jnp.mean(mixed * mixed, axis=1, keepdims=True)) - center * center
    normed = ((mixed - center) * lax.rsqrt(spread + 1e-05)).astype(jnp.bfloat16)
    active = jnp.any(block_ids[:, :, None] == jnp.arange(NBLK, dtype=jnp.int32)[None, None, :], axis=1)
    neuron_mask = jnp.repeat(active.astype(jnp.float32), BLOCK, axis=1)
    upward = jnp.dot(normed, up_weight, preferred_element_type=jnp.float32)
    hidden = (jax.nn.relu(upward) * neuron_mask).astype(jnp.bfloat16)
    feed = jnp.dot(hidden, down_weight, preferred_element_type=jnp.float32)
    return (mixed + feed).astype(jnp.bfloat16)
```

```python
import math

import jax
import jax.numpy as jnp
from jax import lax
from jax.experimental import pallas as pl
from jax.experimental.pallas import tpu as pltpu
from jax.sharding import PartitionSpec as P

HS = 128
BLOCK = 128
EPSILON = 1e-05
CHUNKS = 1
F32 = jnp.float32
BF16 = jnp.bfloat16


def attend_rows(queries, fresh_kv, kv_cache, lengths):
    row_count, width = queries.shape
    heads_here = width // HS
    cache = kv_cache.shape[2]
    shaped_q = queries.reshape(row_count, heads_here, HS)
    cache_keys = kv_cache[0].reshape(row_count, cache, heads_here, HS)
    cache_values = kv_cache[1].reshape(row_count, cache, heads_here, HS)
    scale = 1.0 / math.sqrt(HS)
    scores = jnp.einsum("rhd,rphd->rhp", shaped_q, cache_keys, preferred_element_type=F32) * scale
    positions = jnp.arange(cache)
    visible = positions[None, None, :] < lengths[:, None, None]
    scores = jnp.where(visible, scores, -jnp.inf)
    own_score = (
        jnp.einsum(
            "rhd,rhd->rh",
            shaped_q,
            fresh_kv[0].reshape(row_count, heads_here, HS),
            preferred_element_type=F32,
        )
        * scale
    )
    top = jnp.maximum(jnp.max(scores, axis=2), own_score)
    weights = jnp.exp(scores - top[:, :, None])
    own_weight = jnp.exp(own_score - top)
    total = jnp.sum(weights, axis=2) + own_weight
    probs = (weights / total[:, :, None]).astype(BF16)
    own_prob = (own_weight / total).astype(BF16)
    result = jnp.einsum("rhp,rphd->rhd", probs, cache_values, preferred_element_type=F32)
    result = result + own_prob.astype(F32)[:, :, None] * fresh_kv[1].reshape(
        row_count, heads_here, HS
    ).astype(F32)
    return result.astype(BF16).reshape(row_count, width)


def project_kernel(places, attended, weight, stream, keep, send):
    half, _, width = keep.shape
    values = attended[...]
    for p in range(2 * half):
        columns = pl.ds(pl.multiple_of(places[p] * width, width), width)
        piece = jnp.dot(values, weight[:, columns], preferred_element_type=F32)
        if p == 0:
            piece = piece + stream[...].astype(F32)
        if p < half:
            keep[p] = piece
        else:
            send[p - half] = piece.astype(BF16)


def project(places, attended, weight, stream):
    count, (rows, width) = places.shape[0], stream.shape
    half = count // 2
    if width % 128:
        ordered = weight.reshape(weight.shape[0], count, width)[:, places]
        pieces = jnp.einsum("rk,kpw->prw", attended, ordered, preferred_element_type=F32)
        pieces = pieces.at[0].add(stream.astype(F32))
        return pieces[:half], pieces[half:].astype(BF16)
    return pl.pallas_call(
        project_kernel,
        in_specs=[pl.BlockSpec(memory_space=pltpu.SMEM)] + [pl.BlockSpec(memory_space=pltpu.VMEM)] * 3,
        out_specs=[pl.BlockSpec(memory_space=pltpu.VMEM)] * 2,
        out_shape=[
            jax.ShapeDtypeStruct((half, rows, width), F32),
            jax.ShapeDtypeStruct((half, rows, width), BF16),
        ],
        compiler_params=pltpu.CompilerParams(vmem_limit_bytes=16 * 1024 * 1024),
        cost_estimate=pl.CostEstimate(
            flops=2 * attended.size * count * width, bytes_accessed=weight.size * 2, transcendentals=0
        ),
        name="project",
    )(places, attended, weight, stream)


def feed_kernel(places, first, second, up_own, up_other, down_own, down_other, ids, owners, keep, send):
    half, rows, width = keep.shape
    pieces = [first[p].astype(F32) for p in range(half)] + [second[p].astype(F32) for p in range(half)]
    features = 2 * half * width
    total = sum(jnp.sum(piece, axis=1, keepdims=True) for piece in pieces)
    squares = sum(jnp.sum(piece * piece, axis=1, keepdims=True) for piece in pieces)
    center = total * (1.0 / features)
    spread = squares * (1.0 / features) - center * center
    scale = lax.rsqrt(spread + EPSILON)
    neurons = up_own.shape[1]
    own = jnp.zeros((rows, neurons), F32)
    other = jnp.zeros((rows, neurons), F32)
    for p in range(2 * half):
        normed = ((pieces[p] - center) * scale).astype(BF16)
        span = pl.ds(pl.multiple_of(places[p] * width, width), width)
        own += jnp.dot(normed, up_own[span, :], preferred_element_type=F32)
        other += jnp.dot(normed, up_other[span, :], preferred_element_type=F32)
    named = ids[...]
    blocks = owners[...]
    active = named[:, 0:1] == blocks
    for k in range(1, named.shape[1]):
        active = active | (named[:, k : k + 1] == blocks)
    own = jnp.where(active[:, :neurons], jnp.maximum(own, 0.0), 0.0).astype(BF16)
    other = jnp.where(active[:, neurons:], jnp.maximum(other, 0.0), 0.0).astype(BF16)
    for p in range(2 * half):
        span = pl.ds(pl.multiple_of(places[p] * width, width), width)
        piece = jnp.dot(own, down_own[:, span], preferred_element_type=F32)
        piece += jnp.dot(other, down_other[:, span], preferred_element_type=F32)
        if p < half:
            keep[p] = piece
        else:
            send[p - half] = piece.astype(BF16)


def feed(places, first, second, ups, downs, ids, owners):
    half, rows, width = first.shape
    count = 2 * half
    if width % 128:
        mixed = jnp.concatenate([first, second]).astype(F32)
        center = jnp.mean(mixed, axis=(0, 2), keepdims=True)
        spread = jnp.mean(mixed * mixed, axis=(0, 2), keepdims=True) - center * center
        normed = ((mixed - center) * lax.rsqrt(spread + EPSILON)).astype(BF16)
        upward = [
            jnp.einsum("prw,pwn->rn", normed, up.reshape(count, width, -1)[places], preferred_element_type=F32)
            for up in ups
        ]
        active = jnp.any(ids[:, :, None] == owners[0][None, None, :], axis=1)
        hidden = jnp.where(active, jax.nn.relu(jnp.concatenate(upward, axis=1)), 0.0).astype(BF16)
        down = jnp.concatenate(downs, axis=0).reshape(-1, count, width)[:, places]
        pieces = jnp.einsum("rn,npw->prw", hidden, down, preferred_element_type=F32)
        return pieces[:half], pieces[half:].astype(BF16)
    return pl.pallas_call(
        feed_kernel,
        in_specs=[pl.BlockSpec(memory_space=pltpu.SMEM)] + [pl.BlockSpec(memory_space=pltpu.VMEM)] * 8,
        out_specs=[pl.BlockSpec(memory_space=pltpu.VMEM)] * 2,
        out_shape=[
            jax.ShapeDtypeStruct((half, rows, width), F32),
            jax.ShapeDtypeStruct((half, rows, width), BF16),
        ],
        compiler_params=pltpu.CompilerParams(vmem_limit_bytes=32 * 1024 * 1024),
        cost_estimate=pl.CostEstimate(
            flops=8 * rows * ups[0].size, bytes_accessed=ups[0].size * 8, transcendentals=0
        ),
        name="feed",
    )(places, first, second, *ups, *downs, ids, owners)


def per_device(
    queries, fresh_kv, kv_cache, lengths, stream, out_weight, block_ids, up_weight, down_weight
):
    tensor_count = lax.axis_size("tensor")
    cores = lax.axis_size("request")
    rounds = tensor_count.bit_length() - 1
    tensor, core = lax.axis_index("tensor"), lax.axis_index("request")
    orders = [list(range(rounds)) for _ in range(cores)]
    for c in range(cores):
        if c % 2 and rounds > 1:
            orders[c][0], orders[c][1] = orders[c][1], orders[c][0]

    def swap(array, step):
        pairs = [
            (t * cores + c, (t ^ (1 << orders[c][step])) * cores + c)
            for t in range(tensor_count)
            for c in range(cores)
        ]
        return lax.ppermute(array, ("tensor", "request"), pairs)

    spots = jnp.array(
        [
            [
                sum(((p >> (rounds - 1 - j)) & 1) << orders[c][j] for j in range(rounds))
                for p in range(tensor_count)
            ]
            for c in range(cores)
        ],
        jnp.int32,
    )
    places = spots[core] ^ tensor
    across = [(c, c ^ 1) for c in range(cores)]
    up_other = lax.ppermute(up_weight, "request", across)
    down_other = lax.ppermute(down_weight, "request", across)
    local_blocks = up_weight.shape[1] // BLOCK
    neurons = jnp.arange(local_blocks * BLOCK, dtype=jnp.int32) // BLOCK
    owners = jnp.concatenate(
        [
            (tensor * cores + core) * local_blocks + neurons,
            (tensor * cores + (core ^ 1)) * local_blocks + neurons,
        ]
    )[None, :]
    row_count = queries.shape[0]
    own_ids = lax.dynamic_slice_in_dim(block_ids, core * row_count, row_count, 0)
    attended = attend_rows(queries, fresh_kv, kv_cache, lengths)

    outs = []
    size = row_count // CHUNKS
    for chunk in range(CHUNKS):
        rows = slice(chunk * size, (chunk + 1) * size)
        keep, send = project(places, attended[rows], out_weight, stream[rows])
        for step in range(rounds - 1):
            total = keep + swap(send, step).astype(F32)
            half = total.shape[0] // 2
            if step < rounds - 2:
                keep, send = total[:half], total[half:].astype(BF16)
        got = swap(total.astype(BF16), rounds - 1)
        mixed = total + got[::-1].astype(F32)
        share = mixed[0]
        parts = mixed.astype(BF16)
        for step in range(rounds - 2, 0, -1):
            parts = jnp.concatenate([parts, swap(parts, step)])
        second = swap(parts, 0)
        keep, send = feed(places, parts, second, (up_weight, up_other), (down_weight, down_other), own_ids[rows], owners)
        for step in range(rounds):
            total = keep + swap(send, step).astype(F32)
            half = total.shape[0] // 2
            if half:
                keep, send = total[:half], total[half:].astype(BF16)
        outs.append((share + total[0]).astype(BF16))
    return jnp.concatenate(outs) if CHUNKS > 1 else outs[0]


def solution(mesh):
    in_specs = (
        P(("groups", "request"), "tensor"),
        P(None, ("groups", "request"), "tensor"),
        P(None, ("groups", "request"), None, "tensor"),
        P(("groups", "request")),
        P(("groups", "request"), "tensor"),
        P("tensor", None),
        P("groups", None),
        P(None, ("tensor", "request")),
        P(("tensor", "request"), None),
    )
    out_specs = P(("groups", "request"), "tensor")
    return jax.shard_map(
        per_device, mesh=mesh, in_specs=in_specs, out_specs=out_specs, check_vma=False
    )
```

```python
import functools
import math

import jax
import jax.numpy as jnp
from jax import lax
from jax.experimental import pallas as pl
from jax.experimental.pallas import tpu as pltpu
from jax.sharding import PartitionSpec as P

HS = 128
BLOCK = 128
EPSILON = 1e-05
FOLDS = 2
ONES = 16
MIB = 1024 * 1024
F32 = jnp.float32
BF16 = jnp.bfloat16


def attend_rows(queries, fresh_kv, kv_cache, lengths):
    row_count, width = queries.shape
    heads_here = width // HS
    cache = kv_cache.shape[2]
    shaped_q = queries.reshape(row_count, heads_here, HS)
    cache_keys = kv_cache[0].reshape(row_count, cache, heads_here, HS)
    cache_values = kv_cache[1].reshape(row_count, cache, heads_here, HS)
    scale = 1.0 / math.sqrt(HS)
    scores = jnp.einsum("rhd,rphd->rhp", shaped_q, cache_keys, preferred_element_type=F32) * scale
    positions = jnp.arange(cache)
    visible = positions[None, None, :] < lengths[:, None, None]
    scores = jnp.where(visible, scores, -jnp.inf)
    own_score = (
        jnp.einsum(
            "rhd,rhd->rh",
            shaped_q,
            fresh_kv[0].reshape(row_count, heads_here, HS),
            preferred_element_type=F32,
        )
        * scale
    )
    top = jnp.maximum(jnp.max(scores, axis=2), own_score)
    weights = jnp.exp(scores - top[:, :, None])
    own_weight = jnp.exp(own_score - top)
    total = jnp.sum(weights, axis=2) + own_weight
    probs = (weights / total[:, :, None]).astype(BF16)
    own_prob = (own_weight / total).astype(BF16)
    result = jnp.einsum("rhp,rphd->rhd", probs, cache_values, preferred_element_type=F32)
    result = result + own_prob.astype(F32)[:, :, None] * fresh_kv[1].reshape(
        row_count, heads_here, HS
    ).astype(F32)
    return result.astype(BF16).reshape(row_count, width)


def spot(core, p, count):
    rounds = count.bit_length() - 1
    bits = [(p >> (rounds - 1 - j)) & 1 for j in range(rounds)]
    plain = sum(bit << j for j, bit in enumerate(bits))
    if rounds < 2:
        return plain
    turned = sum(bit << j for j, bit in enumerate([bits[1], bits[0]] + bits[2:]))
    if plain == turned:
        return plain
    return jnp.where(lax.rem(core, 2) == 0, plain, turned)


def span_of(p, fold, count, width):
    place = lax.bitwise_xor(lax.axis_index("tensor"), spot(lax.axis_index("request"), p, count))
    part = width // FOLDS
    return pl.ds(pl.multiple_of(place * width + fold * part, part), part)


def pick(array, axis, p, fold, count, width):
    place = lax.axis_index("tensor") ^ spot(lax.axis_index("request"), p, count)
    part = width // FOLDS
    return lax.dynamic_slice_in_dim(array, place * width + fold * part, part, axis)


def whole(count):
    return [pl.BlockSpec(memory_space=pltpu.VMEM)] * count


def attend_block(queries, fresh_key, fresh_value, keys, values, lengths, base):
    rows, positions = keys.shape[0], keys.shape[1]
    scale = 1.0 / math.sqrt(HS)
    row = lax.broadcasted_iota(jnp.int32, (rows, positions), 0)
    keys = keys.reshape(rows * positions, HS)
    wide = lax.dot_general(queries, keys, (((1,), (1,)), ((), ())), preferred_element_type=F32)
    scores = wide[:, :positions]
    length = jnp.full((rows, positions), lengths[base], jnp.int32)
    for r in range(1, rows):
        scores = jnp.where(row == r, wide[:, r * positions : (r + 1) * positions], scores)
        length = jnp.where(row == r, lengths[base + r], length)
    visible = lax.broadcasted_iota(jnp.int32, (rows, positions), 1) < length
    scores = jnp.where(visible, scores * scale, -jnp.inf)
    own_score = jnp.sum(queries.astype(F32) * fresh_key.astype(F32), axis=1, keepdims=True) * scale
    top = jnp.maximum(jnp.max(scores, axis=1, keepdims=True), own_score)
    weights = jnp.exp(scores - top)
    own_weight = jnp.exp(own_score - top)
    total = jnp.sum(weights, axis=1, keepdims=True) + own_weight
    probs = (weights / total).astype(BF16).astype(F32)
    own_prob = (own_weight / total).astype(BF16).astype(F32)
    spread = jnp.concatenate([jnp.where(row == r, probs, 0.0).astype(BF16) for r in range(rows)], axis=1)
    result = jnp.dot(spread, values.reshape(rows * positions, HS), preferred_element_type=F32)
    return (result + own_prob * fresh_value.astype(F32)).astype(BF16)


def head_kernel(count, step, *refs):
    sources, refs = refs[:7], refs[7:]
    sends, keeps, mask, refs = refs[:FOLDS], refs[FOLDS : 2 * FOLDS], refs[2 * FOLDS], refs[2 * FOLDS + 1 :]
    lengths, queries, fresh, stream, weight, named, cache, turned, sems = refs
    rows, width = stream.shape
    small = [
        pltpu.make_async_copy(source, target, sems.at[i])
        for i, (source, target) in enumerate(zip(sources[:6], (lengths, queries, fresh, stream, weight, named)))
    ]
    blocks = [
        pltpu.make_async_copy(
            sources[6].at[:, pl.ds(i * step, step)], cache.at[:, pl.ds(i * step, step)], sems.at[6 + i]
        )
        for i in range(rows // step)
    ]
    for copy in small[:3] + blocks + small[3:]:
        copy.start()
    for copy in small[:3]:
        copy.wait()
    parts = []
    for i, copy in enumerate(blocks):
        copy.wait()
        span = slice(i * step, (i + 1) * step)
        parts.append(
            attend_block(
                queries[span, :], fresh[0, span, :], fresh[1, span, :], cache[0, span], cache[1, span], lengths, i * step
            )
        )
    attended = jnp.concatenate(parts, axis=0)
    for copy in small[3:]:
        copy.wait()
    half, part = count // 2, width // FOLDS
    for first, outs in ((half, sends), (0, keeps)):
        for fold, out in enumerate(outs):
            for i in range(half):
                span = span_of(first + i, fold, count, width)
                piece = jnp.dot(attended, weight[:, span], preferred_element_type=F32)
                if first + i == 0:
                    piece = piece + stream[:, fold * part : (fold + 1) * part].astype(F32)
                out[i] = piece.astype(out.dtype)
    acts, batch = named.shape
    spare = turned.shape[1] - acts
    ids = named[...].astype(F32)
    if spare:
        ids = jnp.concatenate([ids, jnp.full((spare, batch), -1.0, F32)], axis=0)
    turned[...] = jnp.transpose(ids)
    core, cores = lax.axis_index("request"), lax.axis_size("request")
    own = turned[pl.ds(pl.multiple_of(core * rows, rows), rows), :]
    neurons = mask.shape[1] // 2
    lane = lax.broadcasted_iota(jnp.int32, (rows, neurons), 1) // BLOCK
    for start, place in ((0, core), (neurons, lax.bitwise_xor(core, 1))):
        owner = lax.axis_index("tensor") * cores + place
        blocks = (lane + owner * (neurons // BLOCK)).astype(F32)
        active = own[:, 0:1] == blocks
        for k in range(1, acts):
            active = active | (own[:, k : k + 1] == blocks)
        mask[:, start : start + neurons] = jnp.where(active, 1.0, 0.0)


def head(count, queries, fresh_kv, kv_cache, lengths, stream, weight, block_ids, neurons):
    rows, width = stream.shape
    positions = kv_cache.shape[2]
    half, part = count // 2, width // FOLDS
    step = 16
    if part % 128 or queries.shape[1] != HS or rows % step or positions % 128:
        attended = attend_rows(queries, fresh_kv, kv_cache, lengths)
        sends, keeps = [], []
        for fold in range(FOLDS):
            pieces = [
                jnp.dot(attended, pick(weight, 1, i, fold, count, width), preferred_element_type=F32)
                for i in range(count)
            ]
            pieces[0] = pieces[0] + stream[:, fold * part : (fold + 1) * part].astype(F32)
            keeps.append(jnp.stack(pieces[:half]))
            sends.append(jnp.stack(pieces[half:]).astype(BF16))
        core, cores = lax.axis_index("request"), lax.axis_size("request")
        local = jnp.arange(neurons, dtype=jnp.int32) // BLOCK
        base = lax.axis_index("tensor") * cores
        owners = jnp.concatenate([(base + place) * (neurons // BLOCK) + local for place in (core, core ^ 1)])
        named = lax.dynamic_slice_in_dim(block_ids, core * rows, rows, 0)
        mask = jnp.any(named[:, :, None] == owners[None, None, :], axis=1).astype(F32)
        return sends, keeps, mask
    shapes = [(half, rows, part)] * FOLDS
    operands = [
        pltpu.with_memory_space_constraint(array, pltpu.HBM)
        for array in (lengths, queries, fresh_kv, stream, weight, block_ids.T, kv_cache)
    ]
    batch, acts = block_ids.shape
    outs = pl.pallas_call(
        functools.partial(head_kernel, count, step),
        in_specs=[pl.BlockSpec(memory_space=pltpu.HBM)] * 7,
        out_specs=whole(2 * FOLDS + 1),
        out_shape=[jax.ShapeDtypeStruct(shape, kind) for kind in (BF16, F32) for shape in shapes]
        + [jax.ShapeDtypeStruct((rows, 2 * neurons), F32)],
        scratch_shapes=[
            pltpu.SMEM(lengths.shape, lengths.dtype),
            pltpu.VMEM(queries.shape, BF16),
            pltpu.VMEM(fresh_kv.shape, BF16),
            pltpu.VMEM(stream.shape, BF16),
            pltpu.VMEM(weight.shape, BF16),
            pltpu.VMEM((acts, batch), block_ids.dtype),
            pltpu.VMEM(kv_cache.shape, BF16),
            pltpu.VMEM((batch, -(-acts // 8) * 8), F32),
            pltpu.SemaphoreType.DMA((6 + rows // step,)),
        ],
        compiler_params=pltpu.CompilerParams(vmem_limit_bytes=16 * MIB),
        cost_estimate=pl.CostEstimate(
            flops=4 * rows * positions * HS + 2 * rows * weight.size,
            bytes_accessed=2 * (kv_cache.size + weight.size),
            transcendentals=rows * positions,
        ),
        name="head",
    )(*operands)
    return list(outs[:FOLDS]), list(outs[FOLDS : 2 * FOLDS]), outs[2 * FOLDS]


def up_kernel(first, folds, count, width, last, rows, *refs):
    pieces = refs[: len(folds)]
    up_own, up_other = refs[len(folds) : len(folds) + 2]
    refs = refs[len(folds) + 2 :]
    neurons = up_own.shape[1]
    extra = jnp.ones((ONES, width // FOLDS), BF16)
    total = squares = own = other = None
    for fold, ref in zip(folds, pieces):
        for i in range(ref.shape[0]):
            piece = ref[i]
            span = span_of(first + i, fold, count, width)
            wide = piece.astype(F32)
            add_total = jnp.sum(wide, axis=1, keepdims=True)
            add_squares = jnp.sum(wide * wide, axis=1, keepdims=True)
            stacked = jnp.concatenate([piece, extra], axis=0)
            add_own = jnp.dot(stacked, up_own[span, :], preferred_element_type=F32)
            add_other = jnp.dot(stacked, up_other[span, :], preferred_element_type=F32)
            if own is None:
                total, squares, own, other = add_total, add_squares, add_own, add_other
            else:
                total, squares = total + add_total, squares + add_squares
                own, other = own + add_own, other + add_other
    if first > 0:
        upward, sums = refs[:2]
        refs = refs[2:]
        own = own + upward[:, :neurons]
        other = other + upward[:, neurons:]
        total = total + sums[:, 0:1]
        squares = squares + sums[:, 1:2]
    if not last:
        upward, sums = refs
        upward[:, :neurons] = own
        upward[:, neurons:] = other
        lane = lax.broadcasted_iota(jnp.int32, (rows, 128), 1)
        sums[...] = jnp.where(lane == 0, total, squares)
        return
    mask, hidden = refs
    features = count * width
    center = total * (1.0 / features)
    spread = squares * (1.0 / features) - center * center
    scale = lax.rsqrt(spread + EPSILON)
    for start, value in ((0, own), (neurons, other)):
        upward = (value[:rows] - center * value[rows : rows + 1]) * scale
        active = mask[:, start : start + neurons] > 0
        hidden[:, start : start + neurons] = jnp.where(active, jnp.maximum(upward, 0.0), 0.0).astype(BF16)


def up(first, folds, count, width, pieces, ups, state, mask):
    amount, rows, part = pieces[0].shape
    neurons = ups[0].shape[1]
    if part % 128:
        for fold, piece in zip(folds, pieces):
            extra = jnp.ones((ONES, part), BF16)
            for i in range(amount):
                wide = piece[i].astype(F32)
                stacked = jnp.concatenate([piece[i], extra], axis=0)
                add = jnp.concatenate(
                    [
                        jnp.dot(
                            stacked,
                            pick(weight, 0, first + i, fold, count, width),
                            preferred_element_type=F32,
                        )
                        for weight in ups
                    ],
                    axis=1,
                )
                sums = jnp.stack([jnp.sum(wide, axis=1), jnp.sum(wide * wide, axis=1)], axis=1)
                state = (add, sums) if state is None else (state[0] + add, state[1] + sums)
        if mask is None:
            return state
        upward, sums = state
        features = count * width
        center = sums[:, 0:1] / features
        scale = lax.rsqrt(sums[:, 1:2] / features - center * center + EPSILON)
        upward = (upward[:rows] - center * upward[rows : rows + 1]) * scale
        return jnp.where(mask > 0, jax.nn.relu(upward), 0.0).astype(BF16)
    last = mask is not None
    operands = list(pieces) + list(ups) + ([] if state is None else list(state)) + ([mask] if last else [])
    if last:
        out_shape = jax.ShapeDtypeStruct((rows, 2 * neurons), BF16)
    else:
        out_shape = [
            jax.ShapeDtypeStruct((rows + ONES, 2 * neurons), F32),
            jax.ShapeDtypeStruct((rows, 128), F32),
        ]
    return pl.pallas_call(
        functools.partial(up_kernel, first, folds, count, width, last, rows),
        in_specs=whole(len(operands)),
        out_specs=whole(1)[0] if last else whole(2),
        out_shape=out_shape,
        compiler_params=pltpu.CompilerParams(vmem_limit_bytes=12 * MIB),
        cost_estimate=pl.CostEstimate(
            flops=4 * rows * neurons * amount * part * len(folds),
            bytes_accessed=4 * neurons * amount * part * len(folds),
            transcendentals=0,
        ),
        name="up",
    )(*operands)


def down_kernel(first, folds, count, width, hidden, down_own, down_other, *outs):
    neurons = down_own.shape[0]
    own, other = hidden[:, :neurons], hidden[:, neurons:]
    for fold, out in zip(folds, outs):
        for i in range(out.shape[0]):
            span = span_of(first + i, fold, count, width)
            piece = jnp.dot(own, down_own[:, span], preferred_element_type=F32)
            piece += jnp.dot(other, down_other[:, span], preferred_element_type=F32)
            out[i] = piece.astype(out.dtype)


def down(first, amount, folds, kind, count, width, hidden, downs):
    rows = hidden.shape[0]
    part = width // FOLDS
    if part % 128:
        both = jnp.concatenate(downs, axis=0)
        return [
            jnp.stack(
                [
                    jnp.dot(hidden, pick(both, 1, first + i, fold, count, width), preferred_element_type=F32)
                    for i in range(amount)
                ]
            ).astype(kind)
            for fold in folds
        ]
    return pl.pallas_call(
        functools.partial(down_kernel, first, folds, count, width),
        in_specs=whole(3),
        out_specs=whole(len(folds)),
        out_shape=[jax.ShapeDtypeStruct((amount, rows, part), kind) for _ in folds],
        compiler_params=pltpu.CompilerParams(vmem_limit_bytes=12 * MIB),
        cost_estimate=pl.CostEstimate(
            flops=2 * rows * hidden.shape[1] * amount * part * len(folds),
            bytes_accessed=2 * hidden.shape[1] * amount * part * len(folds),
            transcendentals=0,
        ),
        name="down",
    )(hidden, *downs)


def per_device(
    queries, fresh_kv, kv_cache, lengths, stream, out_weight, block_ids, up_weight, down_weight
):
    count = lax.axis_size("tensor")
    cores = lax.axis_size("request")
    rounds = count.bit_length() - 1
    half = count // 2
    width = stream.shape[1]
    orders = [list(range(rounds)) for _ in range(cores)]
    for c in range(cores):
        if c % 2 and rounds > 1:
            orders[c][0], orders[c][1] = orders[c][1], orders[c][0]

    def swap(array, step):
        pairs = [
            (t * cores + c, (t ^ (1 << orders[c][step])) * cores + c)
            for t in range(count)
            for c in range(cores)
        ]
        return lax.ppermute(array, ("tensor", "request"), pairs)

    across = [(c, c ^ 1) for c in range(cores)]
    ups = (up_weight, lax.ppermute(up_weight, "request", across))
    downs = (down_weight, lax.ppermute(down_weight, "request", across))
    folds = tuple(range(FOLDS))
    sends, keeps, mask = head(
        count, queries, fresh_kv, kv_cache, lengths, stream, out_weight, block_ids, up_weight.shape[1]
    )
    for step in range(rounds - 1):
        for fold in folds:
            total = keeps[fold] + swap(sends[fold], step).astype(F32)
            left = total.shape[0] // 2
            if step < rounds - 2:
                keeps[fold], sends[fold] = total[:left], total[left:].astype(BF16)
            else:
                keeps[fold], sends[fold] = total, total.astype(BF16)
    shares, parts = [], []
    for fold in folds:
        mixed = keeps[fold] + swap(sends[fold], rounds - 1)[::-1].astype(F32)
        shares.append(mixed[0])
        parts.append(mixed.astype(BF16))
    for step in range(rounds - 2, 0, -1):
        for fold in folds:
            parts[fold] = jnp.concatenate([parts[fold], swap(parts[fold], step)])
    state = up(0, folds, count, width, parts, ups, None, None)
    for fold in folds:
        got = swap(parts[fold], 0)
        state = up(half, (fold,), count, width, [got], ups, state, mask if fold == FOLDS - 1 else None)
    hidden = state
    sends = [down(half, half, (fold,), BF16, count, width, hidden, downs)[0] for fold in folds]
    keeps = list(down(0, half, folds, F32, count, width, hidden, downs))
    for step in range(rounds):
        for fold in folds:
            total = keeps[fold] + swap(sends[fold], step).astype(F32)
            left = total.shape[0] // 2
            keeps[fold] = total[: max(left, 1)]
            if left:
                sends[fold] = total[left:].astype(BF16)
    outs = [(shares[fold] + keeps[fold][0]).astype(BF16) for fold in folds]
    return jnp.concatenate(outs, axis=1)


def solution(mesh):
    in_specs = (
        P(("groups", "request"), "tensor"),
        P(None, ("groups", "request"), "tensor"),
        P(None, ("groups", "request"), None, "tensor"),
        P(("groups", "request")),
        P(("groups", "request"), "tensor"),
        P("tensor", None),
        P("groups", None),
        P(None, ("tensor", "request")),
        P(("tensor", "request"), None),
    )
    out_specs = P(("groups", "request"), "tensor")
    return jax.shard_map(
        per_device, mesh=mesh, in_specs=in_specs, out_specs=out_specs, check_vma=False
    )
```

```python
import functools
import math

import jax
import jax.numpy as jnp
from jax import lax
from jax.experimental import pallas as pl
from jax.experimental.pallas import tpu as pltpu
from jax.sharding import PartitionSpec as P

HS = 128
BLOCK = 128
EPSILON = 1e-05
FOLDS = 1
SPLIT = (2, 2)
ONES = 16
MIB = 1024 * 1024
F32 = jnp.float32
BF16 = jnp.bfloat16


def attend_rows(queries, fresh_kv, kv_cache, lengths):
    row_count, width = queries.shape
    heads_here = width // HS
    cache = kv_cache.shape[2]
    shaped_q = queries.reshape(row_count, heads_here, HS)
    cache_keys = kv_cache[0].reshape(row_count, cache, heads_here, HS)
    cache_values = kv_cache[1].reshape(row_count, cache, heads_here, HS)
    scale = 1.0 / math.sqrt(HS)
    scores = jnp.einsum("rhd,rphd->rhp", shaped_q, cache_keys, preferred_element_type=F32) * scale
    positions = jnp.arange(cache)
    visible = positions[None, None, :] < lengths[:, None, None]
    scores = jnp.where(visible, scores, -jnp.inf)
    own_score = (
        jnp.einsum(
            "rhd,rhd->rh",
            shaped_q,
            fresh_kv[0].reshape(row_count, heads_here, HS),
            preferred_element_type=F32,
        )
        * scale
    )
    top = jnp.maximum(jnp.max(scores, axis=2), own_score)
    weights = jnp.exp(scores - top[:, :, None])
    own_weight = jnp.exp(own_score - top)
    total = jnp.sum(weights, axis=2) + own_weight
    probs = (weights / total[:, :, None]).astype(BF16)
    own_prob = (own_weight / total).astype(BF16)
    result = jnp.einsum("rhp,rphd->rhd", probs, cache_values, preferred_element_type=F32)
    result = result + own_prob.astype(F32)[:, :, None] * fresh_kv[1].reshape(
        row_count, heads_here, HS
    ).astype(F32)
    return result.astype(BF16).reshape(row_count, width)


def spot(core, p, count):
    rounds = count.bit_length() - 1
    bits = [(p >> (rounds - 1 - j)) & 1 for j in range(rounds)]
    plain = sum(bit << j for j, bit in enumerate(bits))
    if rounds < 2:
        return plain
    turned = sum(bit << j for j, bit in enumerate([bits[1], bits[0]] + bits[2:]))
    if plain == turned:
        return plain
    return jnp.where(lax.rem(core, 2) == 0, plain, turned)


def span_of(p, fold, count, width):
    place = lax.bitwise_xor(lax.axis_index("tensor"), spot(lax.axis_index("request"), p, count))
    part = width // FOLDS
    return pl.ds(pl.multiple_of(place * width + fold * part, part), part)


def pick(array, axis, p, fold, count, width):
    place = lax.axis_index("tensor") ^ spot(lax.axis_index("request"), p, count)
    part = width // FOLDS
    return lax.dynamic_slice_in_dim(array, place * width + fold * part, part, axis)


def whole(count):
    return [pl.BlockSpec(memory_space=pltpu.VMEM)] * count


def attend_block(queries, fresh_key, fresh_value, keys, values, lengths, base):
    rows, positions = keys.shape[0], keys.shape[1]
    scale = 1.0 / math.sqrt(HS)
    row = lax.broadcasted_iota(jnp.int32, (rows, positions), 0)
    keys = keys.reshape(rows * positions, HS)
    wide = lax.dot_general(queries, keys, (((1,), (1,)), ((), ())), preferred_element_type=F32)
    scores = wide[:, :positions]
    length = jnp.full((rows, positions), lengths[base], jnp.int32)
    for r in range(1, rows):
        scores = jnp.where(row == r, wide[:, r * positions : (r + 1) * positions], scores)
        length = jnp.where(row == r, lengths[base + r], length)
    visible = lax.broadcasted_iota(jnp.int32, (rows, positions), 1) < length
    scores = jnp.where(visible, scores * scale, -jnp.inf)
    own_score = jnp.sum(queries.astype(F32) * fresh_key.astype(F32), axis=1, keepdims=True) * scale
    top = jnp.maximum(jnp.max(scores, axis=1, keepdims=True), own_score)
    weights = jnp.exp(scores - top)
    own_weight = jnp.exp(own_score - top)
    total = jnp.sum(weights, axis=1, keepdims=True) + own_weight
    probs = (weights / total).astype(BF16).astype(F32)
    own_prob = (own_weight / total).astype(BF16).astype(F32)
    spread = jnp.concatenate([jnp.where(row == r, probs, 0.0).astype(BF16) for r in range(rows)], axis=1)
    result = jnp.dot(spread, values.reshape(rows * positions, HS), preferred_element_type=F32)
    return (result + own_prob * fresh_value.astype(F32)).astype(BF16)


def head_kernel(count, step, begin, *refs):
    sources, refs = refs[:8], refs[8:]
    sends, keeps, refs = refs[:FOLDS], refs[FOLDS : 2 * FOLDS], refs[2 * FOLDS :]
    mask, carried, refs = refs[0], refs[1], refs[2:]
    lengths, queries, fresh, stream, weight, named, cache, turned, sems = refs
    rows, width = stream.shape
    all_rows = sources[1].shape[0]
    here = pl.ds(begin, rows)
    views = (
        sources[0],
        sources[1].at[here],
        sources[2].at[:, here],
        sources[3].at[here],
        sources[4],
        sources[5],
    )
    small = [
        pltpu.make_async_copy(source, target, sems.at[i])
        for i, (source, target) in enumerate(zip(views, (lengths, queries, fresh, stream, weight, named)))
    ]
    blocks = [
        pltpu.make_async_copy(
            sources[6].at[:, pl.ds(begin + i * step, step)], cache.at[:, pl.ds(i * step, step)], sems.at[6 + i]
        )
        for i in range(rows // step)
    ]
    fetch = pltpu.make_async_copy(sources[7], carried, sems.at[6 + len(blocks)])
    for copy in small[:3] + blocks + small[3:] + [fetch]:
        copy.start()
    for copy in small[:3]:
        copy.wait()
    parts = []
    for i, copy in enumerate(blocks):
        copy.wait()
        span = slice(i * step, (i + 1) * step)
        parts.append(
            attend_block(
                queries[span, :], fresh[0, span, :], fresh[1, span, :], cache[0, span], cache[1, span], lengths, begin + i * step
            )
        )
    attended = jnp.concatenate(parts, axis=0)
    for copy in small[3:]:
        copy.wait()
    half, part = count // 2, width // FOLDS
    for first, outs in ((half, sends), (0, keeps)):
        for fold, out in enumerate(outs):
            for i in range(half):
                span = span_of(first + i, fold, count, width)
                piece = jnp.dot(attended, weight[:, span], preferred_element_type=F32)
                if first + i == 0:
                    piece = piece + stream[:, fold * part : (fold + 1) * part].astype(F32)
                out[i] = piece.astype(out.dtype)
    acts, batch = named.shape
    spare = turned.shape[1] - acts
    ids = named[...].astype(F32)
    if spare:
        ids = jnp.concatenate([ids, jnp.full((spare, batch), -1.0, F32)], axis=0)
    turned[...] = jnp.transpose(ids)
    core, cores = lax.axis_index("request"), lax.axis_size("request")
    own = turned[pl.ds(pl.multiple_of(core * all_rows + begin, step), rows), :]
    neurons = mask.shape[1] // 2
    lane = lax.broadcasted_iota(jnp.int32, (rows, neurons), 1) // BLOCK
    for start, place in ((0, core), (neurons, lax.bitwise_xor(core, 1))):
        owner = lax.axis_index("tensor") * cores + place
        blocks = (lane + owner * (neurons // BLOCK)).astype(F32)
        active = own[:, 0:1] == blocks
        for k in range(1, acts):
            active = active | (own[:, k : k + 1] == blocks)
        mask[:, start : start + neurons] = jnp.where(active, 1.0, 0.0)
    fetch.wait()


def head(count, begin, rows, queries, fresh_kv, kv_cache, lengths, stream, weight, block_ids, neurons, carried):
    all_rows, width = stream.shape
    positions = kv_cache.shape[2]
    half, part = count // 2, width // FOLDS
    step = 16
    if part % 128 or queries.shape[1] != HS or rows % step or positions % 128:
        here = slice(begin, begin + rows)
        attended = attend_rows(queries[here], fresh_kv[:, here], kv_cache[:, here], lengths[here])
        sends, keeps = [], []
        for fold in range(FOLDS):
            pieces = [
                jnp.dot(attended, pick(weight, 1, i, fold, count, width), preferred_element_type=F32)
                for i in range(count)
            ]
            pieces[0] = pieces[0] + stream[here, fold * part : (fold + 1) * part].astype(F32)
            keeps.append(jnp.stack(pieces[:half]))
            sends.append(jnp.stack(pieces[half:]).astype(BF16))
        core, cores = lax.axis_index("request"), lax.axis_size("request")
        local = jnp.arange(neurons, dtype=jnp.int32) // BLOCK
        base = lax.axis_index("tensor") * cores
        owners = jnp.concatenate([(base + place) * (neurons // BLOCK) + local for place in (core, core ^ 1)])
        named = lax.dynamic_slice_in_dim(block_ids, core * all_rows + begin, rows, 0)
        mask = jnp.any(named[:, :, None] == owners[None, None, :], axis=1).astype(F32)
        return sends, keeps, mask, carried
    shapes = [(half, rows, part)] * FOLDS
    operands = [
        pltpu.with_memory_space_constraint(array, pltpu.HBM)
        for array in (lengths, queries, fresh_kv, stream, weight, block_ids.T, kv_cache, carried)
    ]
    batch, acts = block_ids.shape
    outs = pl.pallas_call(
        functools.partial(head_kernel, count, step, begin),
        in_specs=[pl.BlockSpec(memory_space=pltpu.HBM)] * 8,
        out_specs=whole(2 * FOLDS + 2),
        out_shape=[jax.ShapeDtypeStruct(shape, kind) for kind in (BF16, F32) for shape in shapes]
        + [jax.ShapeDtypeStruct((rows, 2 * neurons), F32), jax.ShapeDtypeStruct(carried.shape, BF16)],
        scratch_shapes=[
            pltpu.SMEM(lengths.shape, lengths.dtype),
            pltpu.VMEM((rows, HS), BF16),
            pltpu.VMEM((2, rows, HS), BF16),
            pltpu.VMEM((rows, width), BF16),
            pltpu.VMEM(weight.shape, BF16),
            pltpu.VMEM((acts, batch), block_ids.dtype),
            pltpu.VMEM((2, rows, positions, HS), BF16),
            pltpu.VMEM((batch, -(-acts // 8) * 8), F32),
            pltpu.SemaphoreType.DMA((7 + rows // step,)),
        ],
        compiler_params=pltpu.CompilerParams(vmem_limit_bytes=16 * MIB),
        cost_estimate=pl.CostEstimate(
            flops=4 * rows * positions * HS + 2 * rows * weight.size,
            bytes_accessed=2 * (2 * rows * positions * HS + weight.size),
            transcendentals=rows * positions,
        ),
        name="head",
    )(*operands)
    return list(outs[:FOLDS]), list(outs[FOLDS : 2 * FOLDS]), outs[2 * FOLDS], outs[2 * FOLDS + 1]


def up_kernel(first, folds, count, width, last, rows, *refs):
    pieces = refs[: len(folds)]
    up_own, up_other = refs[len(folds) : len(folds) + 2]
    refs = refs[len(folds) + 2 :]
    neurons = up_own.shape[1]
    extra = jnp.ones((ONES, width // FOLDS), BF16)
    total = squares = own = other = None
    for fold, ref in zip(folds, pieces):
        for i in range(ref.shape[0]):
            piece = ref[i]
            span = span_of(first + i, fold, count, width)
            wide = piece.astype(F32)
            add_total = jnp.sum(wide, axis=1, keepdims=True)
            add_squares = jnp.sum(wide * wide, axis=1, keepdims=True)
            stacked = jnp.concatenate([piece, extra], axis=0)
            add_own = jnp.dot(stacked, up_own[span, :], preferred_element_type=F32)
            add_other = jnp.dot(stacked, up_other[span, :], preferred_element_type=F32)
            if own is None:
                total, squares, own, other = add_total, add_squares, add_own, add_other
            else:
                total, squares = total + add_total, squares + add_squares
                own, other = own + add_own, other + add_other
    if first > 0:
        upward, sums = refs[:2]
        refs = refs[2:]
        own = own + upward[:, :neurons]
        other = other + upward[:, neurons:]
        total = total + sums[:, 0:1]
        squares = squares + sums[:, 1:2]
    if not last:
        upward, sums = refs
        upward[:, :neurons] = own
        upward[:, neurons:] = other
        lane = lax.broadcasted_iota(jnp.int32, (rows, 128), 1)
        sums[...] = jnp.where(lane == 0, total, squares)
        return
    mask, hidden = refs
    features = count * width
    center = total * (1.0 / features)
    spread = squares * (1.0 / features) - center * center
    scale = lax.rsqrt(spread + EPSILON)
    for start, value in ((0, own), (neurons, other)):
        upward = (value[:rows] - center * value[rows : rows + 1]) * scale
        active = mask[:, start : start + neurons] > 0
        hidden[:, start : start + neurons] = jnp.where(active, jnp.maximum(upward, 0.0), 0.0).astype(BF16)


def up(first, folds, count, width, pieces, ups, state, mask):
    amount, rows, part = pieces[0].shape
    neurons = ups[0].shape[1]
    if part % 128:
        for fold, piece in zip(folds, pieces):
            extra = jnp.ones((ONES, part), BF16)
            for i in range(amount):
                wide = piece[i].astype(F32)
                stacked = jnp.concatenate([piece[i], extra], axis=0)
                add = jnp.concatenate(
                    [
                        jnp.dot(
                            stacked,
                            pick(weight, 0, first + i, fold, count, width),
                            preferred_element_type=F32,
                        )
                        for weight in ups
                    ],
                    axis=1,
                )
                sums = jnp.stack([jnp.sum(wide, axis=1), jnp.sum(wide * wide, axis=1)], axis=1)
                state = (add, sums) if state is None else (state[0] + add, state[1] + sums)
        if mask is None:
            return state
        upward, sums = state
        features = count * width
        center = sums[:, 0:1] / features
        scale = lax.rsqrt(sums[:, 1:2] / features - center * center + EPSILON)
        upward = (upward[:rows] - center * upward[rows : rows + 1]) * scale
        return jnp.where(mask > 0, jax.nn.relu(upward), 0.0).astype(BF16)
    last = mask is not None
    operands = list(pieces) + list(ups) + ([] if state is None else list(state)) + ([mask] if last else [])
    if last:
        out_shape = jax.ShapeDtypeStruct((rows, 2 * neurons), BF16)
    else:
        out_shape = [
            jax.ShapeDtypeStruct((rows + ONES, 2 * neurons), F32),
            jax.ShapeDtypeStruct((rows, 128), F32),
        ]
    return pl.pallas_call(
        functools.partial(up_kernel, first, folds, count, width, last, rows),
        in_specs=whole(len(operands)),
        out_specs=whole(1)[0] if last else whole(2),
        out_shape=out_shape,
        compiler_params=pltpu.CompilerParams(vmem_limit_bytes=12 * MIB),
        cost_estimate=pl.CostEstimate(
            flops=4 * rows * neurons * amount * part * len(folds),
            bytes_accessed=4 * neurons * amount * part * len(folds),
            transcendentals=0,
        ),
        name="up",
    )(*operands)


def down_kernel(first, folds, count, width, hidden, down_own, down_other, *outs):
    neurons = down_own.shape[0]
    own, other = hidden[:, :neurons], hidden[:, neurons:]
    for fold, out in zip(folds, outs):
        for i in range(out.shape[0]):
            span = span_of(first + i, fold, count, width)
            piece = jnp.dot(own, down_own[:, span], preferred_element_type=F32)
            piece += jnp.dot(other, down_other[:, span], preferred_element_type=F32)
            out[i] = piece.astype(out.dtype)


def down(first, amount, folds, kind, count, width, hidden, downs):
    rows = hidden.shape[0]
    part = width // FOLDS
    if part % 128:
        both = jnp.concatenate(downs, axis=0)
        return [
            jnp.stack(
                [
                    jnp.dot(hidden, pick(both, 1, first + i, fold, count, width), preferred_element_type=F32)
                    for i in range(amount)
                ]
            ).astype(kind)
            for fold in folds
        ]
    return pl.pallas_call(
        functools.partial(down_kernel, first, folds, count, width),
        in_specs=whole(3),
        out_specs=whole(len(folds)),
        out_shape=[jax.ShapeDtypeStruct((amount, rows, part), kind) for _ in folds],
        compiler_params=pltpu.CompilerParams(vmem_limit_bytes=12 * MIB),
        cost_estimate=pl.CostEstimate(
            flops=2 * rows * hidden.shape[1] * amount * part * len(folds),
            bytes_accessed=2 * hidden.shape[1] * amount * part * len(folds),
            transcendentals=0,
        ),
        name="down",
    )(hidden, *downs)


def per_device(
    queries, fresh_kv, kv_cache, lengths, stream, out_weight, block_ids, up_weight, down_weight
):
    count = lax.axis_size("tensor")
    cores = lax.axis_size("request")
    rounds = count.bit_length() - 1
    half = count // 2
    width = stream.shape[1]
    orders = [list(range(rounds)) for _ in range(cores)]
    for c in range(cores):
        if c % 2 and rounds > 1:
            orders[c][0], orders[c][1] = orders[c][1], orders[c][0]

    def swap(array, step):
        pairs = [
            (t * cores + c, (t ^ (1 << orders[c][step])) * cores + c)
            for t in range(count)
            for c in range(cores)
        ]
        return lax.ppermute(array, ("tensor", "request"), pairs)

    across = [(c, c ^ 1) for c in range(cores)]
    ups = [up_weight, lax.ppermute(up_weight, "request", across)]
    downs = [down_weight, lax.ppermute(down_weight, "request", across)]
    all_rows = queries.shape[0]
    sizes = [all_rows * share // sum(SPLIT) for share in SPLIT]
    folds = tuple(range(FOLDS))
    chains = [(chunk, fold) for chunk in range(len(sizes)) for fold in folds]
    sends, keeps, masks = {}, {}, []
    for chunk in range(len(sizes)):
        holder = downs if chunk else ups
        send, keep, mask, holder[0] = head(
            count,
            sum(sizes[:chunk]),
            sizes[chunk],
            queries,
            fresh_kv,
            kv_cache,
            lengths,
            stream,
            out_weight,
            block_ids,
            up_weight.shape[1],
            holder[0],
        )
        masks.append(mask)
        for fold in folds:
            sends[chunk, fold], keeps[chunk, fold] = send[fold], keep[fold]
    for step in range(rounds - 1):
        for chain in chains:
            total = keeps[chain] + swap(sends[chain], step).astype(F32)
            left = total.shape[0] // 2
            if step < rounds - 2:
                keeps[chain], sends[chain] = total[:left], total[left:].astype(BF16)
            else:
                keeps[chain], sends[chain] = total, total.astype(BF16)
    shares, parts = {}, {}
    for chain in chains:
        mixed = keeps[chain] + swap(sends[chain], rounds - 1)[::-1].astype(F32)
        shares[chain] = mixed[0]
        parts[chain] = mixed.astype(BF16)
    for step in range(rounds - 2, 0, -1):
        for chain in chains:
            parts[chain] = jnp.concatenate([parts[chain], swap(parts[chain], step)])
    gots = {chain: swap(parts[chain], 0) for chain in chains}
    states = [
        up(0, folds, count, width, [parts[chunk, fold] for fold in folds], ups, None, None)
        for chunk in range(len(sizes))
    ]
    first = {fold: gots[0, fold] for fold in folds}
    states, first = lax.optimization_barrier((states, first))
    gots.update({(0, fold): first[fold] for fold in folds})
    for chunk in range(len(sizes)):
        state = states[chunk]
        for fold in folds:
            mask = masks[chunk] if fold == FOLDS - 1 else None
            state = up(half, (fold,), count, width, [gots[chunk, fold]], ups, state, mask)
        for fold in folds:
            sends[chunk, fold] = down(half, half, (fold,), BF16, count, width, state, downs)[0]
        for fold, keep in zip(folds, down(0, half, folds, F32, count, width, state, downs)):
            keeps[chunk, fold] = keep
    for step in range(rounds):
        for chain in chains:
            total = keeps[chain] + swap(sends[chain], step).astype(F32)
            left = total.shape[0] // 2
            keeps[chain] = total[: max(left, 1)]
            if left:
                sends[chain] = total[left:].astype(BF16)
    outs = {chain: (shares[chain] + keeps[chain][0]).astype(BF16) for chain in chains}
    return jnp.concatenate(
        [jnp.concatenate([outs[chunk, fold] for fold in folds], axis=1) for chunk in range(len(sizes))], axis=0
    )


def solution(mesh):
    in_specs = (
        P(("groups", "request"), "tensor"),
        P(None, ("groups", "request"), "tensor"),
        P(None, ("groups", "request"), None, "tensor"),
        P(("groups", "request")),
        P(("groups", "request"), "tensor"),
        P("tensor", None),
        P("groups", None),
        P(None, ("tensor", "request")),
        P(("tensor", "request"), None),
    )
    out_specs = P(("groups", "request"), "tensor")
    return jax.shard_map(
        per_device, mesh=mesh, in_specs=in_specs, out_specs=out_specs, check_vma=False
    )
```

```python
import functools
import math

import jax
import jax.numpy as jnp
from jax import lax
from jax.experimental import pallas as pl
from jax.experimental.pallas import tpu as pltpu
from jax.sharding import PartitionSpec as P

HS = 128
BLOCK = 128
EPSILON = 1e-05
FOLDS = 1
SPLIT = (2, 2)
ONES = 16
MIB = 1024 * 1024
F32 = jnp.float32
BF16 = jnp.bfloat16


def attend_rows(queries, fresh_kv, kv_cache, lengths):
    row_count, width = queries.shape
    heads_here = width // HS
    cache = kv_cache.shape[2]
    shaped_q = queries.reshape(row_count, heads_here, HS)
    cache_keys = kv_cache[0].reshape(row_count, cache, heads_here, HS)
    cache_values = kv_cache[1].reshape(row_count, cache, heads_here, HS)
    scale = 1.0 / math.sqrt(HS)
    scores = jnp.einsum("rhd,rphd->rhp", shaped_q, cache_keys, preferred_element_type=F32) * scale
    positions = jnp.arange(cache)
    visible = positions[None, None, :] < lengths[:, None, None]
    scores = jnp.where(visible, scores, -jnp.inf)
    own_score = (
        jnp.einsum(
            "rhd,rhd->rh",
            shaped_q,
            fresh_kv[0].reshape(row_count, heads_here, HS),
            preferred_element_type=F32,
        )
        * scale
    )
    top = jnp.maximum(jnp.max(scores, axis=2), own_score)
    weights = jnp.exp(scores - top[:, :, None])
    own_weight = jnp.exp(own_score - top)
    total = jnp.sum(weights, axis=2) + own_weight
    probs = (weights / total[:, :, None]).astype(BF16)
    own_prob = (own_weight / total).astype(BF16)
    result = jnp.einsum("rhp,rphd->rhd", probs, cache_values, preferred_element_type=F32)
    result = result + own_prob.astype(F32)[:, :, None] * fresh_kv[1].reshape(
        row_count, heads_here, HS
    ).astype(F32)
    return result.astype(BF16).reshape(row_count, width)


LEADS = (((0, 1, 2), (1, 0, 2)), ((0, 1, 2), (1, 2, 0)), ((0, 1, 2), (0, 1, 2)))


def order_of(core, phase, count):
    rounds = count.bit_length() - 1
    lead = [axis for axis in LEADS[phase][core % 2] if axis < rounds]
    return lead + [axis for axis in range(rounds) if axis not in lead]


def spot(core, p, count, phase):
    rounds = count.bit_length() - 1
    bits = [(p >> (rounds - 1 - j)) & 1 for j in range(rounds)]
    even, odd = [
        sum(bit << axis for bit, axis in zip(bits, order_of(parity, phase, count))) for parity in (0, 1)
    ]
    if even == odd:
        return even
    return jnp.where(lax.rem(core, 2) == 0, even, odd)


def span_of(p, fold, count, width, phase=0):
    place = lax.bitwise_xor(lax.axis_index("tensor"), spot(lax.axis_index("request"), p, count, phase))
    part = width // FOLDS
    return pl.ds(pl.multiple_of(place * width + fold * part, part), part)


def pick(array, axis, p, fold, count, width, phase=0):
    place = lax.axis_index("tensor") ^ spot(lax.axis_index("request"), p, count, phase)
    part = width // FOLDS
    return lax.dynamic_slice_in_dim(array, place * width + fold * part, part, axis)


def whole(count):
    return [pl.BlockSpec(memory_space=pltpu.VMEM)] * count


def attend_block(queries, fresh_key, fresh_value, keys, values, lengths, base):
    rows, positions = keys.shape[0], keys.shape[1]
    scale = 1.0 / math.sqrt(HS)
    row = lax.broadcasted_iota(jnp.int32, (rows, positions), 0)
    keys = keys.reshape(rows * positions, HS)
    wide = lax.dot_general(queries, keys, (((1,), (1,)), ((), ())), preferred_element_type=F32)
    scores = wide[:, :positions]
    length = jnp.full((rows, positions), lengths[base], jnp.int32)
    for r in range(1, rows):
        scores = jnp.where(row == r, wide[:, r * positions : (r + 1) * positions], scores)
        length = jnp.where(row == r, lengths[base + r], length)
    visible = lax.broadcasted_iota(jnp.int32, (rows, positions), 1) < length
    scores = jnp.where(visible, scores * scale, -jnp.inf)
    own_score = jnp.sum(queries.astype(F32) * fresh_key.astype(F32), axis=1, keepdims=True) * scale
    top = jnp.maximum(jnp.max(scores, axis=1, keepdims=True), own_score)
    weights = jnp.exp(scores - top)
    own_weight = jnp.exp(own_score - top)
    total = jnp.sum(weights, axis=1, keepdims=True) + own_weight
    probs = (weights / total).astype(BF16).astype(F32)
    own_prob = (own_weight / total).astype(BF16).astype(F32)
    spread = jnp.concatenate([jnp.where(row == r, probs, 0.0).astype(BF16) for r in range(rows)], axis=1)
    result = jnp.dot(spread, values.reshape(rows * positions, HS), preferred_element_type=F32)
    return (result + own_prob * fresh_value.astype(F32)).astype(BF16)


def head_kernel(count, step, begin, *refs):
    sources, refs = refs[:7], refs[7:]
    sends, keeps, refs = refs[:FOLDS], refs[FOLDS : 2 * FOLDS], refs[2 * FOLDS :]
    mask, refs = refs[0], refs[1:]
    lengths, queries, fresh, stream, weight, named, cache, turned, sems = refs
    rows, width = stream.shape
    all_rows = sources[1].shape[0]
    here = pl.ds(begin, rows)
    views = (
        sources[0],
        sources[1].at[here],
        sources[2].at[:, here],
        sources[3].at[here],
        sources[4],
        sources[5],
    )
    small = [
        pltpu.make_async_copy(source, target, sems.at[i])
        for i, (source, target) in enumerate(zip(views, (lengths, queries, fresh, stream, weight, named)))
    ]
    blocks = [
        pltpu.make_async_copy(
            sources[6].at[:, pl.ds(begin + i * step, step)], cache.at[:, pl.ds(i * step, step)], sems.at[6 + i]
        )
        for i in range(rows // step)
    ]
    for copy in small[:3] + blocks + small[3:]:
        copy.start()
    for copy in small[:3]:
        copy.wait()
    parts = []
    for i, copy in enumerate(blocks):
        copy.wait()
        span = slice(i * step, (i + 1) * step)
        parts.append(
            attend_block(
                queries[span, :], fresh[0, span, :], fresh[1, span, :], cache[0, span], cache[1, span], lengths, begin + i * step
            )
        )
    attended = jnp.concatenate(parts, axis=0)
    for copy in small[3:]:
        copy.wait()
    half, part = count // 2, width // FOLDS
    for first, outs in ((half, sends), (0, keeps)):
        for fold, out in enumerate(outs):
            for i in range(half):
                span = span_of(first + i, fold, count, width)
                piece = jnp.dot(attended, weight[:, span], preferred_element_type=F32)
                if first + i == 0:
                    piece = piece + stream[:, fold * part : (fold + 1) * part].astype(F32)
                out[i] = piece.astype(out.dtype)
    acts, batch = named.shape
    spare = turned.shape[1] - acts
    ids = named[...].astype(F32)
    if spare:
        ids = jnp.concatenate([ids, jnp.full((spare, batch), -1.0, F32)], axis=0)
    turned[...] = jnp.transpose(ids)
    core, cores = lax.axis_index("request"), lax.axis_size("request")
    own = turned[pl.ds(pl.multiple_of(core * all_rows + begin, step), rows), :]
    neurons = mask.shape[1] // 2
    lane = lax.broadcasted_iota(jnp.int32, (rows, neurons), 1) // BLOCK
    for start, place in ((0, core), (neurons, lax.bitwise_xor(core, 1))):
        owner = lax.axis_index("tensor") * cores + place
        blocks = (lane + owner * (neurons // BLOCK)).astype(F32)
        active = own[:, 0:1] == blocks
        for k in range(1, acts):
            active = active | (own[:, k : k + 1] == blocks)
        mask[:, start : start + neurons] = jnp.where(active, 1.0, 0.0)


def head(count, begin, rows, queries, fresh_kv, kv_cache, lengths, stream, weight, block_ids, neurons):
    all_rows, width = stream.shape
    positions = kv_cache.shape[2]
    half, part = count // 2, width // FOLDS
    step = 16
    if part % 128 or queries.shape[1] != HS or rows % step or positions % 128:
        here = slice(begin, begin + rows)
        attended = attend_rows(queries[here], fresh_kv[:, here], kv_cache[:, here], lengths[here])
        sends, keeps = [], []
        for fold in range(FOLDS):
            pieces = [
                jnp.dot(attended, pick(weight, 1, i, fold, count, width), preferred_element_type=F32)
                for i in range(count)
            ]
            pieces[0] = pieces[0] + stream[here, fold * part : (fold + 1) * part].astype(F32)
            keeps.append(jnp.stack(pieces[:half]))
            sends.append(jnp.stack(pieces[half:]).astype(BF16))
        core, cores = lax.axis_index("request"), lax.axis_size("request")
        local = jnp.arange(neurons, dtype=jnp.int32) // BLOCK
        base = lax.axis_index("tensor") * cores
        owners = jnp.concatenate([(base + place) * (neurons // BLOCK) + local for place in (core, core ^ 1)])
        named = lax.dynamic_slice_in_dim(block_ids, core * all_rows + begin, rows, 0)
        mask = jnp.any(named[:, :, None] == owners[None, None, :], axis=1).astype(F32)
        return sends, keeps, mask
    shapes = [(half, rows, part)] * FOLDS
    operands = [
        pltpu.with_memory_space_constraint(array, pltpu.HBM)
        for array in (lengths, queries, fresh_kv, stream, weight, block_ids.T, kv_cache)
    ]
    batch, acts = block_ids.shape
    outs = pl.pallas_call(
        functools.partial(head_kernel, count, step, begin),
        in_specs=[pl.BlockSpec(memory_space=pltpu.HBM)] * 7,
        out_specs=whole(2 * FOLDS + 1),
        out_shape=[jax.ShapeDtypeStruct(shape, kind) for kind in (BF16, F32) for shape in shapes]
        + [jax.ShapeDtypeStruct((rows, 2 * neurons), F32)],
        scratch_shapes=[
            pltpu.SMEM(lengths.shape, lengths.dtype),
            pltpu.VMEM((rows, HS), BF16),
            pltpu.VMEM((2, rows, HS), BF16),
            pltpu.VMEM((rows, width), BF16),
            pltpu.VMEM(weight.shape, BF16),
            pltpu.VMEM((acts, batch), block_ids.dtype),
            pltpu.VMEM((2, rows, positions, HS), BF16),
            pltpu.VMEM((batch, -(-acts // 8) * 8), F32),
            pltpu.SemaphoreType.DMA((6 + rows // step,)),
        ],
        compiler_params=pltpu.CompilerParams(vmem_limit_bytes=16 * MIB),
        cost_estimate=pl.CostEstimate(
            flops=4 * rows * positions * HS + 2 * rows * weight.size,
            bytes_accessed=2 * (2 * rows * positions * HS + weight.size),
            transcendentals=rows * positions,
        ),
        name="head",
    )(*operands)
    return list(outs[:FOLDS]), list(outs[FOLDS : 2 * FOLDS]), outs[2 * FOLDS]


def fetch_kernel(source, after, target, sems):
    parts = sems.shape[0]
    size = source.shape[0] // parts
    copies = [
        pltpu.make_async_copy(source.at[pl.ds(i * size, size)], target.at[pl.ds(i * size, size)], sems.at[i])
        for i in range(parts)
    ]
    for copy in copies:
        copy.start()
    for copy in copies:
        copy.wait()


def fetch(array, after):
    if after.shape[-1] % 128:
        return array
    return pl.pallas_call(
        fetch_kernel,
        in_specs=[pl.BlockSpec(memory_space=pltpu.HBM), pl.BlockSpec(memory_space=pl.ANY)],
        out_specs=whole(1)[0],
        out_shape=jax.ShapeDtypeStruct(array.shape, array.dtype),
        scratch_shapes=[pltpu.SemaphoreType.DMA((8,))],
        compiler_params=pltpu.CompilerParams(vmem_limit_bytes=8 * MIB),
        cost_estimate=pl.CostEstimate(flops=0, bytes_accessed=4 * array.size, transcendentals=0),
        name="fetch",
    )(pltpu.with_memory_space_constraint(array, pltpu.HBM), after)


def up_kernel(first, folds, count, width, last, rows, *refs):
    pieces = refs[: len(folds)]
    up_own, up_other = refs[len(folds) : len(folds) + 2]
    refs = refs[len(folds) + 2 :]
    neurons = up_own.shape[1]
    extra = jnp.ones((ONES, width // FOLDS), BF16)
    total = squares = own = other = None
    for fold, ref in zip(folds, pieces):
        for i in range(ref.shape[0]):
            piece = ref[i]
            span = span_of(first + i, fold, count, width, 2)
            wide = piece.astype(F32)
            add_total = jnp.sum(wide, axis=1, keepdims=True)
            add_squares = jnp.sum(wide * wide, axis=1, keepdims=True)
            stacked = jnp.concatenate([piece, extra], axis=0)
            add_own = jnp.dot(stacked, up_own[span, :], preferred_element_type=F32)
            add_other = jnp.dot(stacked, up_other[span, :], preferred_element_type=F32)
            if own is None:
                total, squares, own, other = add_total, add_squares, add_own, add_other
            else:
                total, squares = total + add_total, squares + add_squares
                own, other = own + add_own, other + add_other
    if first > 0:
        upward, sums = refs[:2]
        refs = refs[2:]
        own = own + upward[:, :neurons]
        other = other + upward[:, neurons:]
        total = total + sums[:, 0:1]
        squares = squares + sums[:, 1:2]
    if not last:
        upward, sums = refs
        upward[:, :neurons] = own
        upward[:, neurons:] = other
        lane = lax.broadcasted_iota(jnp.int32, (rows, 128), 1)
        sums[...] = jnp.where(lane == 0, total, squares)
        return
    mask, hidden = refs
    features = count * width
    center = total * (1.0 / features)
    spread = squares * (1.0 / features) - center * center
    scale = lax.rsqrt(spread + EPSILON)
    for start, value in ((0, own), (neurons, other)):
        upward = (value[:rows] - center * value[rows : rows + 1]) * scale
        active = mask[:, start : start + neurons] > 0
        hidden[:, start : start + neurons] = jnp.where(active, jnp.maximum(upward, 0.0), 0.0).astype(BF16)


def up(first, folds, count, width, pieces, ups, state, mask):
    amount, rows, part = pieces[0].shape
    neurons = ups[0].shape[1]
    if part % 128:
        for fold, piece in zip(folds, pieces):
            extra = jnp.ones((ONES, part), BF16)
            for i in range(amount):
                wide = piece[i].astype(F32)
                stacked = jnp.concatenate([piece[i], extra], axis=0)
                add = jnp.concatenate(
                    [
                        jnp.dot(
                            stacked,
                            pick(weight, 0, first + i, fold, count, width, 2),
                            preferred_element_type=F32,
                        )
                        for weight in ups
                    ],
                    axis=1,
                )
                sums = jnp.stack([jnp.sum(wide, axis=1), jnp.sum(wide * wide, axis=1)], axis=1)
                state = (add, sums) if state is None else (state[0] + add, state[1] + sums)
        if mask is None:
            return state
        upward, sums = state
        features = count * width
        center = sums[:, 0:1] / features
        scale = lax.rsqrt(sums[:, 1:2] / features - center * center + EPSILON)
        upward = (upward[:rows] - center * upward[rows : rows + 1]) * scale
        return jnp.where(mask > 0, jax.nn.relu(upward), 0.0).astype(BF16)
    last = mask is not None
    operands = list(pieces) + list(ups) + ([] if state is None else list(state)) + ([mask] if last else [])
    if last:
        out_shape = jax.ShapeDtypeStruct((rows, 2 * neurons), BF16)
    else:
        out_shape = [
            jax.ShapeDtypeStruct((rows + ONES, 2 * neurons), F32),
            jax.ShapeDtypeStruct((rows, 128), F32),
        ]
    return pl.pallas_call(
        functools.partial(up_kernel, first, folds, count, width, last, rows),
        in_specs=whole(len(operands)),
        out_specs=whole(1)[0] if last else whole(2),
        out_shape=out_shape,
        compiler_params=pltpu.CompilerParams(vmem_limit_bytes=12 * MIB),
        cost_estimate=pl.CostEstimate(
            flops=4 * rows * neurons * amount * part * len(folds),
            bytes_accessed=4 * neurons * amount * part * len(folds),
            transcendentals=0,
        ),
        name="up",
    )(*operands)


def down_kernel(first, folds, count, width, hidden, down_own, down_other, *outs):
    neurons = down_own.shape[0]
    own, other = hidden[:, :neurons], hidden[:, neurons:]
    for fold, out in zip(folds, outs):
        for i in range(out.shape[0]):
            span = span_of(first + i, fold, count, width, 1)
            piece = jnp.dot(own, down_own[:, span], preferred_element_type=F32)
            piece += jnp.dot(other, down_other[:, span], preferred_element_type=F32)
            out[i] = piece.astype(out.dtype)


def down(first, amount, folds, kind, count, width, hidden, downs):
    rows = hidden.shape[0]
    part = width // FOLDS
    if part % 128:
        both = jnp.concatenate(downs, axis=0)
        return [
            jnp.stack(
                [
                    jnp.dot(hidden, pick(both, 1, first + i, fold, count, width, 1), preferred_element_type=F32)
                    for i in range(amount)
                ]
            ).astype(kind)
            for fold in folds
        ]
    return pl.pallas_call(
        functools.partial(down_kernel, first, folds, count, width),
        in_specs=whole(3),
        out_specs=whole(len(folds)),
        out_shape=[jax.ShapeDtypeStruct((amount, rows, part), kind) for _ in folds],
        compiler_params=pltpu.CompilerParams(vmem_limit_bytes=12 * MIB),
        cost_estimate=pl.CostEstimate(
            flops=2 * rows * hidden.shape[1] * amount * part * len(folds),
            bytes_accessed=2 * hidden.shape[1] * amount * part * len(folds),
            transcendentals=0,
        ),
        name="down",
    )(hidden, *downs)


def per_device(
    queries, fresh_kv, kv_cache, lengths, stream, out_weight, block_ids, up_weight, down_weight
):
    count = lax.axis_size("tensor")
    cores = lax.axis_size("request")
    rounds = count.bit_length() - 1
    half = count // 2
    width = stream.shape[1]
    def swap(array, step, phase=0):
        pairs = [
            (t * cores + c, (t ^ (1 << order_of(c, phase, count)[step])) * cores + c)
            for t in range(count)
            for c in range(cores)
        ]
        return lax.ppermute(array, ("tensor", "request"), pairs)

    across = [(c, c ^ 1) for c in range(cores)]
    ups = [up_weight, lax.ppermute(up_weight, "request", across)]
    downs = [down_weight, lax.ppermute(down_weight, "request", across)]
    all_rows = queries.shape[0]
    sizes = [all_rows * share // sum(SPLIT) for share in SPLIT]
    folds = tuple(range(FOLDS))
    chains = [(chunk, fold) for chunk in range(len(sizes)) for fold in folds]
    sends, keeps, masks = {}, {}, []
    for chunk in range(len(sizes)):
        send, keep, mask = head(
            count,
            sum(sizes[:chunk]),
            sizes[chunk],
            queries,
            fresh_kv,
            kv_cache,
            lengths,
            stream,
            out_weight,
            block_ids,
            up_weight.shape[1],
        )
        masks.append(mask)
        for fold in folds:
            sends[chunk, fold], keeps[chunk, fold] = send[fold], keep[fold]
    for step in range(rounds - 1):
        for chain in chains:
            got = swap(sends[chain], step)
            if step == 0 and chain == chains[0]:
                downs[0] = fetch(down_weight, got)
            elif step == 0 and chain == chains[1]:
                got, downs[0] = lax.optimization_barrier((got, downs[0]))
            total = keeps[chain] + got.astype(F32)
            left = total.shape[0] // 2
            if step < rounds - 2:
                keeps[chain], sends[chain] = total[:left], total[left:].astype(BF16)
            else:
                keeps[chain], sends[chain] = total, total.astype(BF16)
    shares, parts = {}, {}
    for chain in chains:
        mixed = keeps[chain] + swap(sends[chain], rounds - 1)[::-1].astype(F32)
        shares[chain] = mixed[0]
        parts[chain] = mixed.astype(BF16)
    for step in range(rounds - 2, 0, -1):
        for chain in chains:
            parts[chain] = jnp.concatenate([parts[chain], swap(parts[chain], step, 2)])
    gots = {chain: swap(parts[chain], 0, 2) for chain in chains}
    states = [
        up(0, folds, count, width, [parts[chunk, fold] for fold in folds], ups, None, None)
        for chunk in range(len(sizes))
    ]
    first = {fold: gots[0, fold] for fold in folds}
    states, first = lax.optimization_barrier((states, first))
    gots.update({(0, fold): first[fold] for fold in folds})
    for chunk in range(len(sizes)):
        state = states[chunk]
        for fold in folds:
            mask = masks[chunk] if fold == FOLDS - 1 else None
            state = up(half, (fold,), count, width, [gots[chunk, fold]], ups, state, mask)
        for fold in folds:
            sends[chunk, fold] = down(half, half, (fold,), BF16, count, width, state, downs)[0]
        for fold, keep in zip(folds, down(0, half, folds, F32, count, width, state, downs)):
            keeps[chunk, fold] = keep
    for step in range(rounds):
        for chain in chains:
            total = keeps[chain] + swap(sends[chain], step, 1).astype(F32)
            left = total.shape[0] // 2
            keeps[chain] = total[: max(left, 1)]
            if left:
                sends[chain] = total[left:].astype(BF16)
    outs = {chain: (shares[chain] + keeps[chain][0]).astype(BF16) for chain in chains}
    return jnp.concatenate(
        [jnp.concatenate([outs[chunk, fold] for fold in folds], axis=1) for chunk in range(len(sizes))], axis=0
    )


def solution(mesh):
    in_specs = (
        P(("groups", "request"), "tensor"),
        P(None, ("groups", "request"), "tensor"),
        P(None, ("groups", "request"), None, "tensor"),
        P(("groups", "request")),
        P(("groups", "request"), "tensor"),
        P("tensor", None),
        P("groups", None),
        P(None, ("tensor", "request")),
        P(("tensor", "request"), None),
    )
    out_specs = P(("groups", "request"), "tensor")
    return jax.shard_map(
        per_device, mesh=mesh, in_specs=in_specs, out_specs=out_specs, check_vma=False
    )
```

```python
import functools
import math

import jax
import jax.numpy as jnp
from jax import lax
from jax.experimental import pallas as pl
from jax.experimental.pallas import tpu as pltpu
from jax.sharding import PartitionSpec as P

HS = 128
BLOCK = 128
EPSILON = 1e-05
FOLDS = 1
SPLIT = (2, 2)
ONES = 16
MIB = 1024 * 1024
F32 = jnp.float32
BF16 = jnp.bfloat16


def attend_rows(queries, fresh_kv, kv_cache, lengths):
    row_count, width = queries.shape
    heads_here = width // HS
    cache = kv_cache.shape[2]
    shaped_q = queries.reshape(row_count, heads_here, HS)
    cache_keys = kv_cache[0].reshape(row_count, cache, heads_here, HS)
    cache_values = kv_cache[1].reshape(row_count, cache, heads_here, HS)
    scale = 1.0 / math.sqrt(HS)
    scores = jnp.einsum("rhd,rphd->rhp", shaped_q, cache_keys, preferred_element_type=F32) * scale
    positions = jnp.arange(cache)
    visible = positions[None, None, :] < lengths[:, None, None]
    scores = jnp.where(visible, scores, -jnp.inf)
    own_score = (
        jnp.einsum(
            "rhd,rhd->rh",
            shaped_q,
            fresh_kv[0].reshape(row_count, heads_here, HS),
            preferred_element_type=F32,
        )
        * scale
    )
    top = jnp.maximum(jnp.max(scores, axis=2), own_score)
    weights = jnp.exp(scores - top[:, :, None])
    own_weight = jnp.exp(own_score - top)
    total = jnp.sum(weights, axis=2) + own_weight
    probs = (weights / total[:, :, None]).astype(BF16)
    own_prob = (own_weight / total).astype(BF16)
    result = jnp.einsum("rhp,rphd->rhd", probs, cache_values, preferred_element_type=F32)
    result = result + own_prob.astype(F32)[:, :, None] * fresh_kv[1].reshape(
        row_count, heads_here, HS
    ).astype(F32)
    return result.astype(BF16).reshape(row_count, width)


LEADS = (((0, 1, 2), (1, 0, 2)), ((0, 1, 2), (1, 2, 0)), ((0, 1, 2), (0, 1, 2)))


def order_of(core, phase, count):
    rounds = count.bit_length() - 1
    lead = [axis for axis in LEADS[phase][core % 2] if axis < rounds]
    return lead + [axis for axis in range(rounds) if axis not in lead]


def spot(core, p, count, phase):
    rounds = count.bit_length() - 1
    bits = [(p >> (rounds - 1 - j)) & 1 for j in range(rounds)]
    even, odd = [
        sum(bit << axis for bit, axis in zip(bits, order_of(parity, phase, count))) for parity in (0, 1)
    ]
    if even == odd:
        return even
    return jnp.where(lax.rem(core, 2) == 0, even, odd)


def span_of(p, fold, count, width, phase=0):
    place = lax.bitwise_xor(lax.axis_index("tensor"), spot(lax.axis_index("request"), p, count, phase))
    part = width // FOLDS
    return pl.ds(pl.multiple_of(place * width + fold * part, part), part)


def pick(array, axis, p, fold, count, width, phase=0):
    place = lax.axis_index("tensor") ^ spot(lax.axis_index("request"), p, count, phase)
    part = width // FOLDS
    return lax.dynamic_slice_in_dim(array, place * width + fold * part, part, axis)


def whole(count):
    return [pl.BlockSpec(memory_space=pltpu.VMEM)] * count


def attend_block(queries, fresh_key, fresh_value, keys, values, lengths, base):
    rows, positions = keys.shape[0], keys.shape[1]
    scale = 1.0 / math.sqrt(HS)
    row = lax.broadcasted_iota(jnp.int32, (rows, positions), 0)
    keys = keys.reshape(rows * positions, HS)
    wide = lax.dot_general(queries, keys, (((1,), (1,)), ((), ())), preferred_element_type=F32)
    scores = wide[:, :positions]
    length = jnp.full((rows, positions), lengths[base], jnp.int32)
    for r in range(1, rows):
        scores = jnp.where(row == r, wide[:, r * positions : (r + 1) * positions], scores)
        length = jnp.where(row == r, lengths[base + r], length)
    visible = lax.broadcasted_iota(jnp.int32, (rows, positions), 1) < length
    scores = jnp.where(visible, scores * scale, -jnp.inf)
    own_score = jnp.sum(queries.astype(F32) * fresh_key.astype(F32), axis=1, keepdims=True) * scale
    top = jnp.maximum(jnp.max(scores, axis=1, keepdims=True), own_score)
    weights = jnp.exp(scores - top)
    own_weight = jnp.exp(own_score - top)
    total = jnp.sum(weights, axis=1, keepdims=True) + own_weight
    probs = (weights / total).astype(BF16).astype(F32)
    own_prob = (own_weight / total).astype(BF16).astype(F32)
    spread = jnp.concatenate([jnp.where(row == r, probs, 0.0).astype(BF16) for r in range(rows)], axis=1)
    result = jnp.dot(spread, values.reshape(rows * positions, HS), preferred_element_type=F32)
    return (result + own_prob * fresh_value.astype(F32)).astype(BF16)


def head_kernel(count, step, begin, *refs):
    sources, refs = refs[:7], refs[7:]
    sends, keeps, refs = refs[:FOLDS], refs[FOLDS : 2 * FOLDS], refs[2 * FOLDS :]
    mask, refs = refs[0], refs[1:]
    lengths, queries, fresh, stream, weight, named, cache, turned, sems = refs
    rows, width = stream.shape
    all_rows = sources[1].shape[0]
    here = pl.ds(begin, rows)
    views = (
        sources[0],
        sources[1].at[here],
        sources[2].at[:, here],
        sources[3].at[here],
        sources[4],
        sources[5],
    )
    small = [
        pltpu.make_async_copy(source, target, sems.at[i])
        for i, (source, target) in enumerate(zip(views, (lengths, queries, fresh, stream, weight, named)))
    ]
    blocks = [
        pltpu.make_async_copy(
            sources[6].at[:, pl.ds(begin + i * step, step)], cache.at[:, pl.ds(i * step, step)], sems.at[6 + i]
        )
        for i in range(rows // step)
    ]
    for copy in small[:3] + blocks + small[3:]:
        copy.start()
    for copy in small[:3]:
        copy.wait()
    parts = []
    for i, copy in enumerate(blocks):
        copy.wait()
        span = slice(i * step, (i + 1) * step)
        parts.append(
            attend_block(
                queries[span, :], fresh[0, span, :], fresh[1, span, :], cache[0, span], cache[1, span], lengths, begin + i * step
            )
        )
    attended = jnp.concatenate(parts, axis=0)
    for copy in small[3:]:
        copy.wait()
    half, part = count // 2, width // FOLDS
    keeps[0][...] = attended
    for first, outs in ((half, sends),):
        for fold, out in enumerate(outs):
            for i in range(half):
                span = span_of(first + i, fold, count, width)
                piece = jnp.dot(attended, weight[:, span], preferred_element_type=F32)
                if first + i == 0:
                    piece = piece + stream[:, fold * part : (fold + 1) * part].astype(F32)
                out[i] = piece.astype(out.dtype)
    acts, batch = named.shape
    spare = turned.shape[1] - acts
    ids = named[...].astype(F32)
    if spare:
        ids = jnp.concatenate([ids, jnp.full((spare, batch), -1.0, F32)], axis=0)
    turned[...] = jnp.transpose(ids)
    core, cores = lax.axis_index("request"), lax.axis_size("request")
    own = turned[pl.ds(pl.multiple_of(core * all_rows + begin, step), rows), :]
    neurons = mask.shape[1] // 2
    lane = lax.broadcasted_iota(jnp.int32, (rows, neurons), 1) // BLOCK
    for start, place in ((0, core), (neurons, lax.bitwise_xor(core, 1))):
        owner = lax.axis_index("tensor") * cores + place
        blocks = (lane + owner * (neurons // BLOCK)).astype(F32)
        active = own[:, 0:1] == blocks
        for k in range(1, acts):
            active = active | (own[:, k : k + 1] == blocks)
        mask[:, start : start + neurons] = jnp.where(active, 1.0, 0.0)


def hold_kernel(count, begin, attended, weight, stream, keep):
    half, rows, width = keep.shape
    for i in range(half):
        piece = jnp.dot(attended[...], weight[:, span_of(i, 0, count, width)], preferred_element_type=F32)
        if i == 0:
            piece = piece + stream[begin : begin + rows, :].astype(F32)
        keep[i] = piece


def hold(count, begin, attended, weight, stream):
    rows, width = attended.shape[0], stream.shape[1]
    return pl.pallas_call(
        functools.partial(hold_kernel, count, begin),
        in_specs=whole(3),
        out_specs=whole(1)[0],
        out_shape=jax.ShapeDtypeStruct((count // 2, rows, width), F32),
        compiler_params=pltpu.CompilerParams(vmem_limit_bytes=8 * MIB),
        cost_estimate=pl.CostEstimate(flops=rows * weight.size, bytes_accessed=weight.size, transcendentals=0),
        name="hold",
    )(attended, weight, stream)


def head(count, begin, rows, queries, fresh_kv, kv_cache, lengths, stream, weight, block_ids, neurons):
    all_rows, width = stream.shape
    positions = kv_cache.shape[2]
    half, part = count // 2, width // FOLDS
    step = 16
    if part % 128 or queries.shape[1] != HS or rows % step or positions % 128:
        here = slice(begin, begin + rows)
        attended = attend_rows(queries[here], fresh_kv[:, here], kv_cache[:, here], lengths[here])
        sends, keeps = [], []
        for fold in range(FOLDS):
            pieces = [
                jnp.dot(attended, pick(weight, 1, i, fold, count, width), preferred_element_type=F32)
                for i in range(count)
            ]
            pieces[0] = pieces[0] + stream[here, fold * part : (fold + 1) * part].astype(F32)
            keeps.append(jnp.stack(pieces[:half]))
            sends.append(jnp.stack(pieces[half:]).astype(BF16))
        core, cores = lax.axis_index("request"), lax.axis_size("request")
        local = jnp.arange(neurons, dtype=jnp.int32) // BLOCK
        base = lax.axis_index("tensor") * cores
        owners = jnp.concatenate([(base + place) * (neurons // BLOCK) + local for place in (core, core ^ 1)])
        named = lax.dynamic_slice_in_dim(block_ids, core * all_rows + begin, rows, 0)
        mask = jnp.any(named[:, :, None] == owners[None, None, :], axis=1).astype(F32)
        return sends, keeps, mask
    shapes = [(half, rows, part)] * FOLDS
    operands = [
        pltpu.with_memory_space_constraint(array, pltpu.HBM)
        for array in (lengths, queries, fresh_kv, stream, weight, block_ids.T, kv_cache)
    ]
    batch, acts = block_ids.shape
    outs = pl.pallas_call(
        functools.partial(head_kernel, count, step, begin),
        in_specs=[pl.BlockSpec(memory_space=pltpu.HBM)] * 7,
        out_specs=whole(2 * FOLDS + 1),
        out_shape=[jax.ShapeDtypeStruct(shape, BF16) for shape in shapes + [(rows, HS)]]
        + [jax.ShapeDtypeStruct((rows, 2 * neurons), F32)],
        scratch_shapes=[
            pltpu.SMEM(lengths.shape, lengths.dtype),
            pltpu.VMEM((rows, HS), BF16),
            pltpu.VMEM((2, rows, HS), BF16),
            pltpu.VMEM((rows, width), BF16),
            pltpu.VMEM(weight.shape, BF16),
            pltpu.VMEM((acts, batch), block_ids.dtype),
            pltpu.VMEM((2, rows, positions, HS), BF16),
            pltpu.VMEM((batch, -(-acts // 8) * 8), F32),
            pltpu.SemaphoreType.DMA((6 + rows // step,)),
        ],
        compiler_params=pltpu.CompilerParams(vmem_limit_bytes=16 * MIB),
        cost_estimate=pl.CostEstimate(
            flops=4 * rows * positions * HS + 2 * rows * weight.size,
            bytes_accessed=2 * (2 * rows * positions * HS + weight.size),
            transcendentals=rows * positions,
        ),
        name="head",
    )(*operands)
    return list(outs[:FOLDS]), [hold(count, begin, outs[FOLDS], weight, stream)], outs[2 * FOLDS]


def fetch_kernel(source, after, target, sems):
    parts = sems.shape[0]
    size = source.shape[0] // parts
    copies = [
        pltpu.make_async_copy(source.at[pl.ds(i * size, size)], target.at[pl.ds(i * size, size)], sems.at[i])
        for i in range(parts)
    ]
    for copy in copies:
        copy.start()
    for copy in copies:
        copy.wait()


def fetch(array, after):
    if after.shape[-1] % 128:
        return array
    return pl.pallas_call(
        fetch_kernel,
        in_specs=[pl.BlockSpec(memory_space=pltpu.HBM), pl.BlockSpec(memory_space=pl.ANY)],
        out_specs=whole(1)[0],
        out_shape=jax.ShapeDtypeStruct(array.shape, array.dtype),
        scratch_shapes=[pltpu.SemaphoreType.DMA((8,))],
        compiler_params=pltpu.CompilerParams(vmem_limit_bytes=8 * MIB),
        cost_estimate=pl.CostEstimate(flops=0, bytes_accessed=4 * array.size, transcendentals=0),
        name="fetch",
    )(pltpu.with_memory_space_constraint(array, pltpu.HBM), after)


def up_kernel(first, folds, count, width, last, rows, *refs):
    pieces = refs[: len(folds)]
    up_own, up_other = refs[len(folds) : len(folds) + 2]
    refs = refs[len(folds) + 2 :]
    neurons = up_own.shape[1]
    extra = jnp.ones((ONES, width // FOLDS), BF16)
    total = squares = own = other = None
    for fold, ref in zip(folds, pieces):
        for i in range(ref.shape[0]):
            piece = ref[i]
            span = span_of(first + i, fold, count, width, 2)
            wide = piece.astype(F32)
            add_total = jnp.sum(wide, axis=1, keepdims=True)
            add_squares = jnp.sum(wide * wide, axis=1, keepdims=True)
            stacked = jnp.concatenate([piece, extra], axis=0)
            add_own = jnp.dot(stacked, up_own[span, :], preferred_element_type=F32)
            add_other = jnp.dot(stacked, up_other[span, :], preferred_element_type=F32)
            if own is None:
                total, squares, own, other = add_total, add_squares, add_own, add_other
            else:
                total, squares = total + add_total, squares + add_squares
                own, other = own + add_own, other + add_other
    if first > 0:
        upward, sums = refs[:2]
        refs = refs[2:]
        own = own + upward[:, :neurons]
        other = other + upward[:, neurons:]
        total = total + sums[:, 0:1]
        squares = squares + sums[:, 1:2]
    if not last:
        upward, sums = refs
        upward[:, :neurons] = own
        upward[:, neurons:] = other
        lane = lax.broadcasted_iota(jnp.int32, (rows, 128), 1)
        sums[...] = jnp.where(lane == 0, total, squares)
        return
    mask, hidden = refs
    features = count * width
    center = total * (1.0 / features)
    spread = squares * (1.0 / features) - center * center
    scale = lax.rsqrt(spread + EPSILON)
    for start, value in ((0, own), (neurons, other)):
        upward = (value[:rows] - center * value[rows : rows + 1]) * scale
        active = mask[:, start : start + neurons] > 0
        hidden[:, start : start + neurons] = jnp.where(active, jnp.maximum(upward, 0.0), 0.0).astype(BF16)


def up(first, folds, count, width, pieces, ups, state, mask):
    amount, rows, part = pieces[0].shape
    neurons = ups[0].shape[1]
    if part % 128:
        for fold, piece in zip(folds, pieces):
            extra = jnp.ones((ONES, part), BF16)
            for i in range(amount):
                wide = piece[i].astype(F32)
                stacked = jnp.concatenate([piece[i], extra], axis=0)
                add = jnp.concatenate(
                    [
                        jnp.dot(
                            stacked,
                            pick(weight, 0, first + i, fold, count, width, 2),
                            preferred_element_type=F32,
                        )
                        for weight in ups
                    ],
                    axis=1,
                )
                sums = jnp.stack([jnp.sum(wide, axis=1), jnp.sum(wide * wide, axis=1)], axis=1)
                state = (add, sums) if state is None else (state[0] + add, state[1] + sums)
        if mask is None:
            return state
        upward, sums = state
        features = count * width
        center = sums[:, 0:1] / features
        scale = lax.rsqrt(sums[:, 1:2] / features - center * center + EPSILON)
        upward = (upward[:rows] - center * upward[rows : rows + 1]) * scale
        return jnp.where(mask > 0, jax.nn.relu(upward), 0.0).astype(BF16)
    last = mask is not None
    operands = list(pieces) + list(ups) + ([] if state is None else list(state)) + ([mask] if last else [])
    if last:
        out_shape = jax.ShapeDtypeStruct((rows, 2 * neurons), BF16)
    else:
        out_shape = [
            jax.ShapeDtypeStruct((rows + ONES, 2 * neurons), F32),
            jax.ShapeDtypeStruct((rows, 128), F32),
        ]
    return pl.pallas_call(
        functools.partial(up_kernel, first, folds, count, width, last, rows),
        in_specs=whole(len(operands)),
        out_specs=whole(1)[0] if last else whole(2),
        out_shape=out_shape,
        compiler_params=pltpu.CompilerParams(vmem_limit_bytes=12 * MIB),
        cost_estimate=pl.CostEstimate(
            flops=4 * rows * neurons * amount * part * len(folds),
            bytes_accessed=4 * neurons * amount * part * len(folds),
            transcendentals=0,
        ),
        name="up",
    )(*operands)


def down_kernel(first, folds, count, width, hidden, down_own, down_other, *outs):
    neurons = down_own.shape[0]
    own, other = hidden[:, :neurons], hidden[:, neurons:]
    for fold, out in zip(folds, outs):
        for i in range(out.shape[0]):
            span = span_of(first + i, fold, count, width, 1)
            piece = jnp.dot(own, down_own[:, span], preferred_element_type=F32)
            piece += jnp.dot(other, down_other[:, span], preferred_element_type=F32)
            out[i] = piece.astype(out.dtype)


def down(first, amount, folds, kind, count, width, hidden, downs):
    rows = hidden.shape[0]
    part = width // FOLDS
    if part % 128:
        both = jnp.concatenate(downs, axis=0)
        return [
            jnp.stack(
                [
                    jnp.dot(hidden, pick(both, 1, first + i, fold, count, width, 1), preferred_element_type=F32)
                    for i in range(amount)
                ]
            ).astype(kind)
            for fold in folds
        ]
    return pl.pallas_call(
        functools.partial(down_kernel, first, folds, count, width),
        in_specs=whole(3),
        out_specs=whole(len(folds)),
        out_shape=[jax.ShapeDtypeStruct((amount, rows, part), kind) for _ in folds],
        compiler_params=pltpu.CompilerParams(vmem_limit_bytes=12 * MIB),
        cost_estimate=pl.CostEstimate(
            flops=2 * rows * hidden.shape[1] * amount * part * len(folds),
            bytes_accessed=2 * hidden.shape[1] * amount * part * len(folds),
            transcendentals=0,
        ),
        name="down",
    )(hidden, *downs)


def per_device(
    queries, fresh_kv, kv_cache, lengths, stream, out_weight, block_ids, up_weight, down_weight
):
    count = lax.axis_size("tensor")
    cores = lax.axis_size("request")
    rounds = count.bit_length() - 1
    half = count // 2
    width = stream.shape[1]
    def swap(array, step, phase=0):
        pairs = [
            (t * cores + c, (t ^ (1 << order_of(c, phase, count)[step])) * cores + c)
            for t in range(count)
            for c in range(cores)
        ]
        return lax.ppermute(array, ("tensor", "request"), pairs)

    across = [(c, c ^ 1) for c in range(cores)]
    ups = [up_weight, lax.ppermute(up_weight, "request", across)]
    downs = [down_weight, lax.ppermute(down_weight, "request", across)]
    all_rows = queries.shape[0]
    sizes = [all_rows * share // sum(SPLIT) for share in SPLIT]
    folds = tuple(range(FOLDS))
    chains = [(chunk, fold) for chunk in range(len(sizes)) for fold in folds]
    sends, keeps, masks = {}, {}, []
    for chunk in range(len(sizes)):
        send, keep, mask = head(
            count,
            sum(sizes[:chunk]),
            sizes[chunk],
            queries,
            fresh_kv,
            kv_cache,
            lengths,
            stream,
            out_weight,
            block_ids,
            up_weight.shape[1],
        )
        masks.append(mask)
        for fold in folds:
            sends[chunk, fold], keeps[chunk, fold] = send[fold], keep[fold]
    for step in range(rounds - 1):
        for chain in chains:
            got = swap(sends[chain], step)
            if step == 0 and chain == chains[0]:
                downs[0] = fetch(down_weight, got)
            elif step == 0 and chain == chains[1]:
                got, downs[0] = lax.optimization_barrier((got, downs[0]))
            total = keeps[chain] + got.astype(F32)
            left = total.shape[0] // 2
            if step < rounds - 2:
                keeps[chain], sends[chain] = total[:left], total[left:].astype(BF16)
            else:
                keeps[chain], sends[chain] = total, total.astype(BF16)
    shares, parts = {}, {}
    for chain in chains:
        mixed = keeps[chain] + swap(sends[chain], rounds - 1)[::-1].astype(F32)
        shares[chain] = mixed[0]
        parts[chain] = mixed.astype(BF16)
    for step in range(rounds - 2, 0, -1):
        for chain in chains:
            parts[chain] = jnp.concatenate([parts[chain], swap(parts[chain], step, 2)])
    gots = {chain: swap(parts[chain], 0, 2) for chain in chains}
    states = [
        up(0, folds, count, width, [parts[chunk, fold] for fold in folds], ups, None, None)
        for chunk in range(len(sizes))
    ]
    first = {fold: gots[0, fold] for fold in folds}
    states, first = lax.optimization_barrier((states, first))
    gots.update({(0, fold): first[fold] for fold in folds})
    for chunk in range(len(sizes)):
        state = states[chunk]
        for fold in folds:
            mask = masks[chunk] if fold == FOLDS - 1 else None
            state = up(half, (fold,), count, width, [gots[chunk, fold]], ups, state, mask)
        for fold in folds:
            sends[chunk, fold] = down(half, half, (fold,), BF16, count, width, state, downs)[0]
        for fold, keep in zip(folds, down(0, half, folds, F32, count, width, state, downs)):
            keeps[chunk, fold] = keep
    for step in range(rounds):
        for chain in chains:
            total = keeps[chain] + swap(sends[chain], step, 1).astype(F32)
            left = total.shape[0] // 2
            keeps[chain] = total[: max(left, 1)]
            if left:
                sends[chain] = total[left:].astype(BF16)
    outs = {chain: (shares[chain] + keeps[chain][0]).astype(BF16) for chain in chains}
    return jnp.concatenate(
        [jnp.concatenate([outs[chunk, fold] for fold in folds], axis=1) for chunk in range(len(sizes))], axis=0
    )


def solution(mesh):
    in_specs = (
        P(("groups", "request"), "tensor"),
        P(None, ("groups", "request"), "tensor"),
        P(None, ("groups", "request"), None, "tensor"),
        P(("groups", "request")),
        P(("groups", "request"), "tensor"),
        P("tensor", None),
        P("groups", None),
        P(None, ("tensor", "request")),
        P(("tensor", "request"), None),
    )
    out_specs = P(("groups", "request"), "tensor")
    return jax.shard_map(
        per_device, mesh=mesh, in_specs=in_specs, out_specs=out_specs, check_vma=False
    )
```
